256 devices in a mesh: row: 16 (over y, z_lo), col: 16 (over x, z_hi, core).
Axes of the slice: x: 4, y: 4, z: 8 (z_hi: 2, z_lo: 4; z = z_hi * 4 + z_lo), core: 2. Of those that a mesh axis runs over, the one named last changes fastest.
Arguments:
- activations: bfloat16 [2048, 28672], P('col', 'row'), may hold values from -36 to 36
- output_gradient: bfloat16 [2048, 8192], P('row', 'col'), may hold values from -6 to 6
- frozen_weight: bfloat16 [28672, 8192], P('row', 'col'), may hold values from -0.0390625 to 0.0390625
- sparsity_mask_pattern: int32 [7168, 8192], P('row', 'col'), may hold values from 0 to 5
- adapter_left_factor: bfloat16 [28672, 16], P('row'), may hold values from -0.19921875 to 0.19921875
- adapter_right_factor: bfloat16 [16, 8192], P(None, 'col'), may hold values from -0.359375 to 0.359375
Outputs:
- input_grad: bfloat16 [2048, 28672], P('col', 'row')
- left_grad: float32 [28672, 16], P('row')
- right_grad: float32 [16, 8192], P(None, 'col')
The draws below stay inside these ranges and needn't reach their ends.
Inputs may be any that keep to these rules, and one draw needn't show every extreme that they name: `sparsity_mask_pattern`: a pattern number of the 2:4 mask.
All inputs are finite; a program needn't handle non-finite values.
Results may differ from the reference program's by a relative error of at most 0.005.
Values may be sent and summed in bfloat16 or wider, within the bound.
A program may use at most 64 MiB of HBM per device.

```python
import jax
import jax.numpy as jnp
from jax import lax

MODEL_WIDTH = 8192
HIDDEN_UNITS = 28672
ADAPTER_RANK = 16
TOKENS = 2048
N_ROW = 16


def plant(drawn, stream_key, least, high):
    dims = drawn.shape
    place = [jax.random.randint(jax.random.fold_in(stream_key, axis), (), 0, dims[axis]) for axis in range(len(dims))]
    drawn = drawn.at[tuple(place)].set(least)
    longest = dims.index(max(dims))
    place[longest] = (place[longest] + 1) % dims[longest]
    return drawn.at[tuple(place)].set(high)


def raised(drawn, key, source, target, shards_of, factor):
    owner, partner = [(jnp.arange(drawn.shape[position]) // (drawn.shape[position] // shards_of)).reshape([-1 if axis == position else 1 for axis in range(drawn.ndim)]) for position in (source, target)]
    chosen = jax.random.permutation(key, shards_of)[partner]
    strong = (owner == chosen) | (owner == (partner + shards_of // 2) % shards_of)
    return jnp.where(strong, factor * drawn, drawn)


def levels(stream_key, shape, split, smallest, largest):
    factor_of, own = 1.0, jax.random.fold_in(stream_key, 6)
    for dim, blocks in split:
        steps = jnp.exp(jax.random.uniform(jax.random.fold_in(own, dim), (blocks,), jnp.float32, smallest / len(split), largest / len(split)))
        factor_of = factor_of * jnp.repeat(steps, shape[dim] // blocks).reshape([-1 if axis == dim else 1 for axis in range(len(shape))])
    return factor_of


def noise(key, extent, spread, reach, shards=(), dtype=jnp.bfloat16):
    drawn = spread * jax.random.normal(key, extent, jnp.float32)
    if shards:
        drawn = drawn * levels(key, extent, shards, -0.22, 0.18)
    return jnp.clip(drawn, -reach, reach).astype(dtype)


def bell_draw_with(key, dims, width, most, cuts, heavy, held_as=jnp.bfloat16):
    drawn = width * jax.random.normal(key, dims, jnp.float32)
    if cuts:
        drawn = drawn * levels(key, dims, cuts, -0.22, 0.18)
    return jnp.clip(raised(drawn, jax.random.fold_in(key, 3), *heavy), -most, most).astype(held_as)


def setup_inputs(seed: int = 0) -> dict:
    streams_of = jax.random.split(jax.random.key(seed), 7)
    activations = noise(streams_of[0], (TOKENS, HIDDEN_UNITS), 6.0, 36.0, ((0, 16), (1, 16)))
    output_gradient = bell_draw_with(streams_of[1], (TOKENS, MODEL_WIDTH), 1.0, 6.0, ((0, 16), (1, 16)), (1, 0, 16, 2.0))
    frozen_weight = noise(streams_of[2], (HIDDEN_UNITS, MODEL_WIDTH), (3 * HIDDEN_UNITS // 4) ** -0.5, 0.0390625, ((0, 16), (1, 16)))
    sparsity_mask_pattern = plant(jax.random.randint(streams_of[3], (HIDDEN_UNITS // 4, MODEL_WIDTH), 0, 6), jax.random.fold_in(streams_of[3], 1), 0, 5).astype(jnp.int32)
    adapter_left_factor = noise(streams_of[4], (HIDDEN_UNITS, ADAPTER_RANK), 0.032, 0.19921875, ((0, 16),))
    adapter_right_factor = noise(streams_of[5], (ADAPTER_RANK, MODEL_WIDTH), 0.06, 0.359375, ((1, 16),))
    return dict(activations=activations, output_gradient=output_gradient, frozen_weight=frozen_weight, sparsity_mask_pattern=sparsity_mask_pattern, adapter_left_factor=adapter_left_factor, adapter_right_factor=adapter_right_factor)


PAIRS = ((0, 1), (0, 2), (0, 3), (1, 2), (1, 3), (2, 3))
ADAPTER_SCALE = 2.0


def expand_mask(code):
    groups = []
    for column in range(4):
        kept = jnp.zeros(code.shape, jnp.float32)
        for pattern in range(6):
            if column in PAIRS[pattern]:
                kept = kept + (code == pattern).astype(jnp.float32)
        groups.append(kept)
    stacked = jnp.stack(groups, axis=1)
    return stacked.reshape(code.shape[0] * 4, code.shape[1])


def reference(activations, output_gradient, frozen_weight, sparsity_mask_pattern, adapter_left_factor, adapter_right_factor):
    block_list = N_ROW
    width_extent = HIDDEN_UNITS // block_list
    act_blocks = activations.reshape(TOKENS, block_list, width_extent).transpose(1, 0, 2)
    weight_blocks = frozen_weight.reshape(block_list, width_extent, MODEL_WIDTH)
    code_blocks = sparsity_mask_pattern.reshape(block_list, width_extent // 4, MODEL_WIDTH)
    left_block_list = adapter_left_factor.reshape(block_list, width_extent, ADAPTER_RANK)

    def one_block(carry, inputs):
        act_piece, weight_piece, code_piece, left_block_slice = inputs
        masked = expand_mask(code_piece)
        low_rank_update = jnp.dot(left_block_slice, adapter_right_factor, preferred_element_type=jnp.float32)
        merged = (masked * (weight_piece.astype(jnp.float32) + ADAPTER_SCALE * low_rank_update)).astype(jnp.bfloat16)
        input_piece = lax.dot_general(output_gradient, merged, (((1,), (1,)), ((), ())), preferred_element_type=jnp.float32).astype(jnp.bfloat16)
        weight_grad = lax.dot_general(act_piece, output_gradient, (((0,), (0,)), ((), ())), preferred_element_type=jnp.float32)
        pruned_gradient = (masked * weight_grad / TOKENS).astype(jnp.bfloat16)
        left_slice_gradient = ADAPTER_SCALE * lax.dot_general(pruned_gradient, adapter_right_factor, (((1,), (1,)), ((), ())), preferred_element_type=jnp.float32)
        carry = carry + ADAPTER_SCALE * lax.dot_general(left_block_slice, pruned_gradient, (((0,), (0,)), ((), ())), preferred_element_type=jnp.float32)
        return carry, (input_piece, left_slice_gradient)

    start_carry = jnp.zeros((ADAPTER_RANK, MODEL_WIDTH), jnp.float32)
    right_grad, outputs = lax.scan(one_block, start_carry, (act_blocks, weight_blocks, code_blocks, left_block_list))
    input_parts, left_parts = outputs
    input_grad = input_parts.transpose(1, 0, 2).reshape(TOKENS, HIDDEN_UNITS)
    left_grad = left_parts.reshape(HIDDEN_UNITS, ADAPTER_RANK)
    return input_grad, left_grad, right_grad
```

```python
import functools

import jax
import jax.numpy as jnp
from jax import lax
from jax.experimental import pallas as pl
from jax.experimental.pallas import tpu as pltpu
from jax.sharding import PartitionSpec as P

MESH = pl.DeviceIdType.MESH
BF16, F32 = jnp.bfloat16, jnp.float32
TOKENS, RANK = 2048, 16
TOK, HID, COLS = 128, 1792, 512
HALF, BOTH = HID // 2, 2 * COLS
NT = (((1,), (1,)), ((), ()))
TN = (((0,), (0,)), ((), ()))
HT = 128
WIDE = ((0, 256), (256, 256), (512, 256), (768, 128))

NUMBERS = {}


def numbered(name, count):
    NUMBERS[name] = sum(c for _, c in NUMBERS.values()), count


for _name, _count in (
    ("AX", 4), ("AZ", 2), ("AS", 1), ("AF", 2), ("AP", 4), ("APF", 2),
    ("GZ", 3), ("GY", 8), ("GF", 4), ("GS", 16),
    ("W", 1), ("C", 1), ("R", 1),
    ("S1", 4), ("S2", 4), ("S3", 4), ("Z", 1), ("O", 1),
    ("LX", 3), ("LZ", 3), ("RC", 1), ("RY", 3), ("RZ", 3),
):
    numbered(_name, _count)
COPIES = sum(c for _, c in NUMBERS.values())


def number(name, index=0):
    return NUMBERS[name][0] + index


def merge_tiles(slot, w_buf, c_buf, r_buf, l_buf, mask_buf, m_buf):
    cols = pl.ds(slot * COLS, COLS)
    groups = HT // 4
    row = lax.broadcasted_iota(jnp.int32, (HT, HT), 0)
    lane = lax.broadcasted_iota(jnp.int32, (HT, HT), 1)
    hit = (row % 4 == lane // groups) & (row // 4 == lane % groups)
    spread = jnp.where(hit, 1.0, 0.0).astype(BF16)
    right = r_buf[:, cols]

    def tile(i, _):
        code = c_buf[pl.ds(pl.multiple_of(i * groups, groups), groups), cols]
        is0, is1, is2 = code == 0, code == 1, code == 2
        is3, is4, is5 = code == 3, code == 4, code == 5
        kept = (is0 | is1 | is2, is0 | is3 | is4, is1 | is3 | is5, is2 | is4 | is5)
        kept = jnp.concatenate([jnp.where(b, 1.0, 0.0) for b in kept], axis=0).astype(BF16)
        mask = jnp.dot(spread, kept, preferred_element_type=F32)
        rows = pl.ds(pl.multiple_of(i * HT, HT), HT)
        low = jnp.dot(l_buf[rows, :], right, preferred_element_type=F32)
        merged = mask * (w_buf[rows, cols].astype(F32) + 2.0 * low)
        mask_buf[rows, cols] = mask.astype(BF16)
        m_buf[rows, cols] = merged.astype(BF16)
        return 0

    lax.fori_loop(0, HALF // HT, tile, 0)


def product(i, x_dest, g_buf, m_buf, p_buf):
    first = pl.multiple_of(x_dest * 4 * TOK, 4 * TOK)
    for at, size in WIDE:
        p_buf[i, :, at : at + size] = lax.dot_general(
            g_buf[pl.ds(first, 4 * TOK), :], m_buf[at : at + size, :], NT, preferred_element_type=F32
        )


def turn(a_buf, at_buf, first, count):
    def block(i, _):
        toks = pl.ds(pl.multiple_of(i * TOK, TOK), TOK)
        at_buf[:, toks] = a_buf[toks, :].T
        return 0

    lax.fori_loop(first, first + count, block, 0)


def factor_grads(at_buf, g_buf, mask_buf, r_buf, l_buf, left, right):
    left[...] = jnp.zeros_like(left)
    step = 256

    def tile(n, _):
        cols = pl.ds(pl.multiple_of(n * step, step), step)
        total = jnp.zeros((RANK, step), F32)
        for half in range(2):
            rows = pl.ds(half * (HALF // 2), HALF // 2)
            grad = jnp.dot(at_buf[rows, :], g_buf[:, cols], preferred_element_type=F32)
            pruned = (mask_buf[rows, cols].astype(F32) * grad * (1.0 / TOKENS)).astype(BF16)
            total += lax.dot_general(l_buf[rows, :], pruned, TN, preferred_element_type=F32)
            left[half] += 2.0 * lax.dot_general(
                r_buf[:, cols], pruned, NT, preferred_element_type=F32
            )
        right[:, cols] = 2.0 * total
        return 0

    lax.fori_loop(0, BOTH // step, tile, 0)


def kernel(
    a, g, w, code, lf, rf, out, left_out, right_out,
    a_buf, at_buf, g_buf, w_buf, c_buf, r_buf, l_buf, mask_buf, m_buf,
    p_buf, s_buf, got1, got2, z_send, z_got, o_send, o_own,
    lpart, lx, lz, lgot, rpart, rgot, ry, rz,
    send_sem, recv_sem, local_sem,
):
    row, col = lax.axis_index("row"), lax.axis_index("col")
    y, zl = row // 4, row % 4
    x, zh, k = col // 4, (col // 2) % 2, col % 2
    other = 1 - zh

    def device(y_=y, zl_=zl, x_=x, zh_=zh, k_=k):
        return (y_ * 4 + zl_, x_ * 4 + zh_ * 2 + k_)

    def wrap(v):
        return v % 4

    x_at = (wrap(x + 1), wrap(x + 3))
    y_at = (wrap(y + 1), wrap(y + 3))
    sibling = device(k_=1 - k)
    peers = [sibling]
    peers += [device(x_=x_at[d], k_=j) for d in range(2) for j in range(2)]
    peers += [device(x_=wrap(x + 2))]
    peers += [device(zh_=other, k_=j) for j in range(2)]
    peers += [device(y_=wrap(y + i)) for i in range(1, 4)]
    peers += [device(zl_=wrap(zl + i)) for i in range(1, 4)]

    pending = []

    def send(src, dst, n, to, recv_n=None):
        copy = pltpu.make_async_remote_copy(
            src_ref=src, dst_ref=dst, send_sem=send_sem.at[n],
            recv_sem=recv_sem.at[n if recv_n is None else recv_n],
            device_id=to, device_id_type=MESH,
        )
        copy.start()
        pending.append(copy)

    def arrived(dst, n):
        pltpu.make_async_remote_copy(
            src_ref=dst, dst_ref=dst, send_sem=send_sem.at[n], recv_sem=recv_sem.at[n],
            device_id=sibling, device_id_type=MESH,
        ).wait_recv()

    def tokens_of(x_, zh_, k_):
        return pl.ds(pl.multiple_of((x_ * 4 + zh_ * 2 + k_) * TOK, TOK), TOK)

    def a_block(x_, zh_, k_):
        return a_buf.at[tokens_of(x_, zh_, k_), :]

    def g_block(y_, zl_, slot=0):
        return g_buf.at[pl.ds(pl.multiple_of((y_ * 4 + zl_) * TOK, TOK), TOK), pl.ds(slot * COLS, COLS)]

    def half(j):
        return pl.ds(pl.multiple_of(j * HALF, HALF), HALF)

    def quarter(j):
        return pl.ds(pl.multiple_of(j * (HALF // 4), HALF // 4), HALF // 4)

    own_cols, sib_cols = pl.ds(0, COLS), pl.ds(COLS, COLS)

    locals_ = [
        pltpu.make_async_copy(src, dst, local_sem.at[n])
        for n, (src, dst) in enumerate((
            (w.at[half(k), :], w_buf.at[:, own_cols]),
            (code.at[quarter(k), :], c_buf.at[:, own_cols]),
            (lf.at[half(k), :], l_buf),
            (rf, r_buf.at[:, own_cols]),
            (a.at[:, half(k)], a_block(x, zh, k)),
            (g, g_block(y, zl)),
        ))
    ]
    for copy in locals_:
        copy.start()

    barrier = pltpu.get_barrier_semaphore()
    for peer in peers:
        pl.semaphore_signal(barrier, inc=1, device_id=peer, device_id_type=MESH)
    pl.semaphore_wait(barrier, len(peers))

    for j in range(2):
        for d in range(2):
            send(a.at[:, half(j)], a_block(x, zh, k), number("AX", 2 * d + j), device(x_=x_at[d], k_=j),
                 number("AX", 2 * d) + k)
    for d in range(2):
        send(g, g_block(y, zl), number("GY", 4 * d), device(y_=y_at[d]))
    for i in range(1, 4):
        send(g, g_block(y, zl), number("GZ", i - 1), device(zl_=wrap(zl + i)))
    send(rf, r_buf.at[:, sib_cols], number("R"), sibling)
    send(code.at[quarter(1 - k), :], c_buf.at[:, sib_cols], number("C"), sibling)
    send(w.at[half(1 - k), :], w_buf.at[:, sib_cols], number("W"), sibling)
    send(g, g_block(y, zl, 1), number("GS"), sibling)
    for i in range(2):
        j = k if i == 0 else 1 - k
        send(a.at[:, half(j)], a_block(x, zh, k), number("AZ", i), device(zh_=other, k_=j), number("AZ") + k)
    send(a.at[:, half(1 - k)], a_block(x, zh, k), number("AS"), sibling)

    for copy in locals_:
        copy.wait()
    merge_tiles(0, w_buf, c_buf, r_buf, l_buf, mask_buf, m_buf)

    def g_to_sibling(n, y_, zl_):
        send(g_block(y_, zl_), g_block(y_, zl_, 1), number("GS", n), sibling)

    def a_forward(name, base, zh_):
        for d in range(2):
            block = a_block(x_at[1 - d], zh_, d)
            arrived(block, number(base, 2 * d + d))
            send(block, block, number(name, d), device(x_=x_at[d]))

    def g_from_y(i):
        for d in range(2):
            from_y, from_zl = y_at[1 - d], wrap(zl + 4 - i)
            block = g_block(from_y, from_zl)
            arrived(block, number("GY", 4 * d + i))
            if i % 2 == d:
                send(block, block, number("GF", i), device(y_=y_at[d]))
            g_to_sibling(4 + 4 * d + i, from_y, from_zl)

    g_from_y(0)
    a_forward("AF", "AX", zh)
    for i in range(1, 4):
        block = g_block(y, wrap(zl + 4 - i))
        arrived(block, number("GZ", i - 1))
        for d in range(2):
            send(block, block, number("GY", 4 * d + i), device(y_=y_at[d]))
        g_to_sibling(i, y, wrap(zl + 4 - i))
    for name, ref in (("R", r_buf), ("C", c_buf), ("W", w_buf)):
        arrived(ref.at[:, sib_cols], number(name))
    merge_tiles(1, w_buf, c_buf, r_buf, l_buf, mask_buf, m_buf)
    for i in range(1, 4):
        g_from_y(i)
    for o in range(2):
        block = a_block(x, other, o)
        arrived(block, number("AZ", o))
        for d in range(2):
            send(block, block, number("AP", 2 * d + o), device(x_=x_at[d]))
    for i in range(4):
        block = g_block(wrap(y + 2), wrap(zl + 4 - i))
        arrived(block, number("GF", i))
        g_to_sibling(12 + i, wrap(y + 2), wrap(zl + 4 - i))
    arrived(g_block(y, zl, 1), number("GS"))
    for i in range(1, 4):
        arrived(g_block(y, wrap(zl + 4 - i), 1), number("GS", i))
    for d in range(2):
        for i in range(4):
            arrived(g_block(y_at[1 - d], wrap(zl + 4 - i), 1), number("GS", 4 + 4 * d + i))
    for i in range(4):
        arrived(g_block(wrap(y + 2), wrap(zl + 4 - i), 1), number("GS", 12 + i))

    def part(zh_, h):
        return pl.ds(pl.multiple_of(zh_ * 2 * TOK + h * TOK, TOK), TOK)

    zs = (other, zh)

    product(0, wrap(x + 2), g_buf, m_buf, p_buf)
    s_buf[0] = p_buf[0].astype(BF16)
    for q, zh_ in enumerate(zs):
        for d in range(2):
            send(s_buf.at[0, part(zh_, d), :], got1.at[d, zh_], number("S1", 2 * q + d), device(x_=x_at[d]),
                 number("S1", d) + 2 * zh_)
    a_forward("APF", "AP", other)
    for d in range(2):
        product(1 + d, x_at[d], g_buf, m_buf, p_buf)
        for q, zh_ in enumerate(zs):
            rows = part(zh_, 1 - d)
            s_buf[1 + d, rows, :] = p_buf[1 + d, rows, :].astype(BF16)
            send(s_buf.at[1 + d, rows, :], got2.at[d, rows, :], number("S2", 2 * q + d), device(x_=x_at[d]),
                 number("S2", d) + 2 * zh_)
    product(3, x, g_buf, m_buf, p_buf)
    for q, zh_ in enumerate(zs):
        for d in range(2):
            arrived(got1.at[d, zh_], number("S1", d) + 2 * zh_)
            rows = part(zh_, d)
            s_buf[1 + d, rows, :] = (p_buf[1 + d, rows, :] + got1[d, zh_].astype(F32)).astype(BF16)
            send(s_buf.at[1 + d, rows, :], got2.at[d, rows, :], number("S3", 2 * q + d), device(x_=x_at[d]),
                 number("S3", d) + 2 * zh_)

    arrived(a_block(x, zh, 1 - k), number("AS"))
    for d in range(2):
        arrived(a_block(x_at[1 - d], zh, 1 - d), number("AX", 2 * d + 1 - d))
        arrived(a_block(wrap(x + 2), zh, d), number("AF", d))
        arrived(a_block(x_at[1 - d], other, 1 - d), number("AP", 2 * d + 1 - d))
        arrived(a_block(wrap(x + 2), other, d), number("APF", d))
    turn(a_buf, at_buf, 0, TOKENS // TOK)
    factor_grads(at_buf, g_buf, mask_buf, r_buf, l_buf, lpart, rpart)
    for i in range(2):
        lx[x, :, i * (HALF // 2) : (i + 1) * (HALF // 2)] = lpart[i]
    for i in range(1, 4):
        send(lx.at[x], lx.at[x], number("LX", i - 1), device(x_=wrap(x + i)))
    send(rpart.at[:, sib_cols], rgot, number("RC"), sibling)

    def summed(q, zh_):
        rows = pl.ds(pl.multiple_of(zh_ * 2 * TOK, 2 * TOK), 2 * TOK)
        for d in range(2):
            arrived(got2.at[d, part(zh_, 1 - d), :], number("S2", d) + 2 * zh_)
            arrived(got2.at[d, part(zh_, d), :], number("S3", d) + 2 * zh_)
        return p_buf[3, rows, :] + got2[0, rows, :].astype(F32) + got2[1, rows, :].astype(F32)

    z_send[...] = summed(0, other).astype(BF16)
    send(z_send, z_got, number("Z"), device(zh_=other))

    arrived(rgot, number("RC"))
    ry[y] = rpart[:, :COLS] + rgot[...]
    for i in range(1, 4):
        send(ry.at[y], ry.at[y], number("RY", i - 1), device(y_=wrap(y + i)))
    for i in range(1, 4):
        arrived(lx.at[wrap(x + 4 - i)], number("LX", i - 1))
    lz[...] = (lx[0] + lx[1]) + (lx[2] + lx[3])
    for i, to in enumerate((device(zh_=other), sibling, device(zh_=other, k_=1 - k))):
        send(lz, lgot.at[i], number("LZ", i), to)
    for i in range(1, 4):
        arrived(ry.at[wrap(y + 4 - i)], number("RY", i - 1))
    rz[zl] = (ry[0] + ry[1]) + (ry[2] + ry[3])
    for i in range(1, 4):
        send(rz.at[zl], rz.at[zl], number("RZ", i - 1), device(zl_=wrap(zl + i)))
    for i in range(3):
        arrived(lgot.at[i], number("LZ", i))
    left_out[:, half(k)] = lz[...] + lgot[0]
    left_out[:, half(1 - k)] = lgot[1] + lgot[2]
    for i in range(1, 4):
        arrived(rz.at[wrap(zl + 4 - i)], number("RZ", i - 1))
    right_out[...] = (rz[0] + rz[1]) + (rz[2] + rz[3])

    p_buf[0, : 2 * TOK, :] = summed(1, zh)
    arrived(z_got, number("Z"))
    theirs = pl.ds(pl.multiple_of((1 - k) * TOK, TOK), TOK)
    ours = pl.ds(pl.multiple_of(k * TOK, TOK), TOK)
    o_send[...] = (p_buf[0, theirs, :] + z_got[theirs, :].astype(F32)).astype(BF16)
    send(o_send, out.at[:, half(k)], number("O"), sibling)
    o_own[...] = (p_buf[0, ours, :] + z_got[ours, :].astype(F32)).astype(BF16)
    last = pltpu.make_async_copy(o_own, out.at[:, half(k)], local_sem.at[0])
    last.start()
    last.wait()
    arrived(out.at[:, half(1 - k)], number("O"))
    for copy in pending:
        copy.wait_send()


def per_device(a, g, w, code, lf, rf):
    anywhere = pl.BlockSpec(memory_space=pl.ANY)
    vmem = pl.BlockSpec(memory_space=pltpu.VMEM)
    out, left, right = pl.pallas_call(
        kernel,
        out_shape=(
            jax.ShapeDtypeStruct((TOK, HID), BF16),
            jax.ShapeDtypeStruct((RANK, HID), F32),
            jax.ShapeDtypeStruct((RANK, COLS), F32),
        ),
        in_specs=[anywhere] * 6,
        out_specs=(anywhere, vmem, vmem),
        scratch_shapes=[
            pltpu.VMEM((TOKENS, HALF), BF16),
            pltpu.VMEM((HALF, TOKENS), BF16),
            pltpu.VMEM((TOKENS, BOTH), BF16),
            pltpu.VMEM((HALF, BOTH), BF16),
            pltpu.VMEM((HALF // 4, BOTH), jnp.int32),
            pltpu.VMEM((RANK, BOTH), BF16),
            pltpu.VMEM((HALF, RANK), BF16),
            pltpu.VMEM((HALF, BOTH), BF16),
            pltpu.VMEM((HALF, BOTH), BF16),
            pltpu.VMEM((4, 4 * TOK, HALF), F32),
            pltpu.VMEM((3, 4 * TOK, HALF), BF16),
            pltpu.VMEM((2, 2, TOK, HALF), BF16),
            pltpu.VMEM((2, 4 * TOK, HALF), BF16),
            pltpu.VMEM((2 * TOK, HALF), BF16),
            pltpu.VMEM((2 * TOK, HALF), BF16),
            pltpu.VMEM((TOK, HALF), BF16),
            pltpu.VMEM((TOK, HALF), BF16),
            pltpu.VMEM((2, RANK, HALF // 2), F32),
            pltpu.VMEM((4, RANK, HALF), F32),
            pltpu.VMEM((RANK, HALF), F32),
            pltpu.VMEM((3, RANK, HALF), F32),
            pltpu.VMEM((RANK, BOTH), F32),
            pltpu.VMEM((RANK, COLS), F32),
            pltpu.VMEM((4, RANK, COLS), F32),
            pltpu.VMEM((4, RANK, COLS), F32),
            pltpu.SemaphoreType.DMA((COPIES,)),
            pltpu.SemaphoreType.DMA((COPIES,)),
            pltpu.SemaphoreType.DMA((6,)),
        ],
        compiler_params=pltpu.CompilerParams(
            collective_id=0, has_side_effects=True, vmem_limit_bytes=58 << 20
        ),
        cost_estimate=pl.CostEstimate(flops=7_600_000_000, bytes_accessed=5_000_000, transcendentals=0),
        name="down_projection_backward",
    )(a, g, w, code, lf, rf)
    return out, left.T, right


def solution(mesh):
    in_specs = (
        P("col", "row"),
        P("row", "col"),
        P("row", "col"),
        P("row", "col"),
        P("row", None),
        P(None, "col"),
    )
    out_specs = (P("col", "row"), P("row", None), P(None, "col"))
    return jax.shard_map(
        per_device, mesh=mesh, in_specs=in_specs, out_specs=out_specs, check_vma=False
    )
```

```python
import functools

import jax
import jax.numpy as jnp
from jax import lax
from jax.experimental import pallas as pl
from jax.experimental.pallas import tpu as pltpu
from jax.sharding import PartitionSpec as P

MESH = pl.DeviceIdType.MESH
BF16, F32 = jnp.bfloat16, jnp.float32
TOKENS, RANK = 2048, 16
TOK, HID, COLS = 128, 1792, 512
HALF, BOTH = HID // 2, 2 * COLS
NT = (((1,), (1,)), ((), ()))
TN = (((0,), (0,)), ((), ()))
HT = 128
PIECE = TOK // 2
WIDE = ((0, 256), (256, 256), (512, 256), (768, 128))

NUMBERS = {}


def numbered(name, count):
    NUMBERS[name] = sum(c for _, c in NUMBERS.values()), count


for _name, _count in (
    ("AX", 4), ("AZ", 2), ("AS", 1), ("AF", 2), ("AP", 4), ("APF", 2),
    ("GZ", 3), ("GY", 8), ("GF", 4), ("GS", 16),
    ("W", 1), ("C", 1), ("R", 1),
    ("S1", 8), ("S2", 8), ("S3", 8), ("Z", 2), ("O", 2),
    ("LX", 3), ("LZ", 3), ("RC", 1), ("RY", 3), ("RZ", 3),
):
    numbered(_name, _count)
COPIES = sum(c for _, c in NUMBERS.values())


def number(name, index=0):
    return NUMBERS[name][0] + index


def merge_tiles(slot, w_buf, c_buf, r_buf, l_buf, mask_buf, m_buf):
    cols = pl.ds(slot * COLS, COLS)
    groups = HT // 4
    row = lax.broadcasted_iota(jnp.int32, (HT, HT), 0)
    lane = lax.broadcasted_iota(jnp.int32, (HT, HT), 1)
    hit = (row % 4 == lane // groups) & (row // 4 == lane % groups)
    spread = jnp.where(hit, 1.0, 0.0).astype(BF16)
    right = r_buf[:, cols]

    def tile(i, _):
        code = c_buf[pl.ds(pl.multiple_of(i * groups, groups), groups), cols]
        is0, is1, is2 = code == 0, code == 1, code == 2
        is3, is4, is5 = code == 3, code == 4, code == 5
        kept = (is0 | is1 | is2, is0 | is3 | is4, is1 | is3 | is5, is2 | is4 | is5)
        kept = jnp.concatenate([jnp.where(b, 1.0, 0.0) for b in kept], axis=0).astype(BF16)
        mask = jnp.dot(spread, kept, preferred_element_type=F32)
        rows = pl.ds(pl.multiple_of(i * HT, HT), HT)
        low = lax.dot_general(l_buf[:, rows], right, TN, preferred_element_type=F32)
        merged = mask * (w_buf[rows, cols].astype(F32) + 2.0 * low)
        mask_buf[rows, cols] = mask.astype(BF16)
        m_buf[rows, cols] = merged.astype(BF16)
        return 0

    lax.fori_loop(0, HALF // HT, tile, 0)


def product(i, x_dest, g_buf, m_buf, p_buf):
    first = pl.multiple_of(x_dest * 4 * TOK, 4 * TOK)
    for at, size in WIDE:
        p_buf[i, :, at : at + size] = lax.dot_general(
            g_buf[pl.ds(first, 4 * TOK), :], m_buf[at : at + size, :], NT, preferred_element_type=F32
        )


def turn(a_buf, at_buf, first, count):
    def block(i, _):
        toks = pl.ds(pl.multiple_of(i * TOK, TOK), TOK)
        at_buf[:, toks] = a_buf[toks, :].T
        return 0

    lax.fori_loop(first, first + count, block, 0)


def factor_grads(at_buf, g_buf, mask_buf, r_buf, l_buf, left, right):
    left[...] = jnp.zeros_like(left)
    step = 256

    def tile(n, _):
        cols = pl.ds(pl.multiple_of(n * step, step), step)
        total = jnp.zeros((RANK, step), F32)
        for half in range(2):
            rows = pl.ds(half * (HALF // 2), HALF // 2)
            grad = jnp.dot(at_buf[rows, :], g_buf[:, cols], preferred_element_type=F32)
            pruned = (mask_buf[rows, cols].astype(F32) * grad * (1.0 / TOKENS)).astype(BF16)
            total += jnp.dot(l_buf[:, rows], pruned, preferred_element_type=F32)
            left[half] += 2.0 * lax.dot_general(
                r_buf[:, cols], pruned, NT, preferred_element_type=F32
            )
        right[:, cols] = 2.0 * total
        return 0

    lax.fori_loop(0, BOTH // step, tile, 0)


def kernel(
    a, g, w, code, lf, rf, out, left_out, right_out,
    a_buf, at_buf, g_buf, w_buf, c_buf, r_buf, l_buf, mask_buf, m_buf,
    p_buf, s_buf, got1, got2, z_send, z_got, o_send, o_own,
    lpart, lx, lz, lgot, rpart, rgot, ry, rz,
    send_sem, recv_sem, local_sem,
):
    row, col = lax.axis_index("row"), lax.axis_index("col")
    y, zl = row // 4, row % 4
    x, zh, k = col // 4, (col // 2) % 2, col % 2
    other = 1 - zh

    def device(y_=y, zl_=zl, x_=x, zh_=zh, k_=k):
        return (y_ * 4 + zl_, x_ * 4 + zh_ * 2 + k_)

    def wrap(v):
        return v % 4

    x_at = (wrap(x + 1), wrap(x + 3))
    y_at = (wrap(y + 1), wrap(y + 3))
    sibling = device(k_=1 - k)
    peers = [sibling]
    peers += [device(x_=x_at[d], k_=j) for d in range(2) for j in range(2)]
    peers += [device(x_=wrap(x + 2))]
    peers += [device(zh_=other, k_=j) for j in range(2)]
    peers += [device(y_=wrap(y + i)) for i in range(1, 4)]
    peers += [device(zl_=wrap(zl + i)) for i in range(1, 4)]

    pending = {}

    def send(src, dst, n, to, recv_n=None):
        copy = pltpu.make_async_remote_copy(
            src_ref=src, dst_ref=dst, send_sem=send_sem.at[n],
            recv_sem=recv_sem.at[n if recv_n is None else recv_n],
            device_id=to, device_id_type=MESH,
        )
        copy.start()
        pending[n] = copy

    def arrived(dst, n):
        pltpu.make_async_remote_copy(
            src_ref=dst, dst_ref=dst, send_sem=send_sem.at[n], recv_sem=recv_sem.at[n],
            device_id=sibling, device_id_type=MESH,
        ).wait_recv()

    def sent(n):
        pending.pop(n).wait_send()

    def tokens_of(x_, zh_, k_):
        return pl.ds(pl.multiple_of((x_ * 4 + zh_ * 2 + k_) * TOK, TOK), TOK)

    def a_block(x_, zh_, k_):
        return a_buf.at[tokens_of(x_, zh_, k_), :]

    def g_block(y_, zl_, slot=0):
        return g_buf.at[pl.ds(pl.multiple_of((y_ * 4 + zl_) * TOK, TOK), TOK), pl.ds(slot * COLS, COLS)]

    def half(j):
        return pl.ds(pl.multiple_of(j * HALF, HALF), HALF)

    def quarter(j):
        return pl.ds(pl.multiple_of(j * (HALF // 4), HALF // 4), HALF // 4)

    own_cols, sib_cols = pl.ds(0, COLS), pl.ds(COLS, COLS)

    locals_ = [
        pltpu.make_async_copy(src, dst, local_sem.at[n])
        for n, (src, dst) in enumerate((
            (w.at[half(k), :], w_buf.at[:, own_cols]),
            (code.at[quarter(k), :], c_buf.at[:, own_cols]),
            (lf.at[:, half(k)], l_buf),
            (rf, r_buf.at[:, own_cols]),
            (a.at[:, half(k)], a_block(x, zh, k)),
            (g, g_block(y, zl)),
        ))
    ]
    for copy in locals_:
        copy.start()

    barrier = pltpu.get_barrier_semaphore()
    for peer in peers:
        pl.semaphore_signal(barrier, inc=1, device_id=peer, device_id_type=MESH)
    pl.semaphore_wait(barrier, len(peers))

    def send_a_x():
        for j in range(2):
            for d in range(2):
                send(a.at[:, half(j)], a_block(x, zh, k), number("AX", 2 * d + j), device(x_=x_at[d], k_=j),
                     number("AX", 2 * d) + k)

    def send_g():
        for d in range(2):
            send(g, g_block(y, zl), number("GY", 4 * d), device(y_=y_at[d]))
        for i in (1, 3, 2):
            send(g, g_block(y, zl), number("GZ", i - 1), device(zl_=wrap(zl + i)))

    def send_a_z(i):
        j = k if i == 0 else 1 - k
        send(a.at[:, half(j)], a_block(x, zh, k), number("AZ", i), device(zh_=other, k_=j), number("AZ") + k)

    def send_sibling():
        send(g, g_block(y, zl, 1), number("GS"), sibling)
        send(rf, r_buf.at[:, sib_cols], number("R"), sibling)
        send(code.at[quarter(1 - k), :], c_buf.at[:, sib_cols], number("C"), sibling)
        send(w.at[half(1 - k), :], w_buf.at[:, sib_cols], number("W"), sibling)
        send(a.at[:, half(1 - k)], a_block(x, zh, k), number("AS"), sibling)

    def merge_own():
        for copy in locals_:
            copy.wait()
        merge_tiles(0, w_buf, c_buf, r_buf, l_buf, mask_buf, m_buf)

    def merge_sibling():
        for name, ref in (("R", r_buf), ("C", c_buf), ("W", w_buf)):
            arrived(ref.at[:, sib_cols], number(name))
        merge_tiles(1, w_buf, c_buf, r_buf, l_buf, mask_buf, m_buf)

    def g_to_sibling(n, y_, zl_):
        send(g_block(y_, zl_), g_block(y_, zl_, 1), number("GS", n), sibling)

    def a_forward(name, base, zh_, d):
        block = a_block(x_at[1 - d], zh_, d)
        arrived(block, number(base, 2 * d + d))
        send(block, block, number(name, d), device(x_=x_at[d]))

    def a_from_z(i):
        o = k if i == 0 else 1 - k
        block = a_block(x, other, o)
        arrived(block, number("AZ") + o)
        for d in range(2):
            send(block, block, number("AP", 2 * d + i), device(x_=x_at[d]), number("AP", 2 * d) + o)

    def g_from_z(i):
        block = g_block(y, wrap(zl + 4 - i))
        arrived(block, number("GZ", i - 1))
        for d in range(2):
            send(block, block, number("GY", 4 * d + i), device(y_=y_at[d]))
        g_to_sibling(i, y, wrap(zl + 4 - i))

    def g_from_y(i):
        for d in (i % 2, 1 - i % 2):
            from_y, from_zl = y_at[1 - d], wrap(zl + 4 - i)
            block = g_block(from_y, from_zl)
            arrived(block, number("GY", 4 * d + i))
            if i % 2 == d:
                send(block, block, number("GF", i), device(y_=y_at[d]))
            g_to_sibling(4 + 4 * d + i, from_y, from_zl)

    def g_from_far(i):
        block = g_block(wrap(y + 2), wrap(zl + 4 - i))
        arrived(block, number("GF", i))
        g_to_sibling(12 + i, wrap(y + 2), wrap(zl + 4 - i))

    def g_all():
        for i in range(4):
            arrived(g_block(y, wrap(zl + 4 - i), 1), number("GS", i))
        for d in range(2):
            for i in range(4):
                arrived(g_block(y_at[1 - d], wrap(zl + 4 - i), 1), number("GS", 4 + 4 * d + i))
        for i in range(4):
            arrived(g_block(wrap(y + 2), wrap(zl + 4 - i), 1), number("GS", 12 + i))

    def piece(zh_, h, u):
        return pl.ds(pl.multiple_of(zh_ * 2 * TOK + h * TOK + u * PIECE, PIECE), PIECE)

    def share_number(name, zh_, u, d):
        return number(name) + (zh_ * 4 + u * 2 + d)

    def send_far(q, u):
        zh_ = zs[q]
        for d in range(2):
            rows = piece(zh_, d, u)
            s_buf[0, rows, :] = p_buf[0, rows, :].astype(BF16)
            send(s_buf.at[0, rows, :], got1.at[d, rows, :], number("S1", 4 * q + 2 * u + d),
                 device(x_=x_at[d]), share_number("S1", zh_, u, d))

    def send_near(q, u, d):
        zh_ = zs[q]
        rows = piece(zh_, 1 - d, u)
        s_buf[1 + d, rows, :] = p_buf[1 + d, rows, :].astype(BF16)
        send(s_buf.at[1 + d, rows, :], got2.at[d, rows, :], number("S2", 4 * q + 2 * u + d),
             device(x_=x_at[d]), share_number("S2", zh_, u, d))

    def pass_on(q, u):
        zh_ = zs[q]
        for d in range(2):
            rows = piece(zh_, d, u)
            arrived(got1.at[d, rows, :], share_number("S1", zh_, u, d))
            s_buf[1 + d, rows, :] = (p_buf[1 + d, rows, :] + got1[d, rows, :].astype(F32)).astype(BF16)
            send(s_buf.at[1 + d, rows, :], got2.at[d, rows, :], number("S3", 4 * q + 2 * u + d),
                 device(x_=x_at[d]), share_number("S3", zh_, u, d))

    def summed(q, u, h):
        zh_ = zs[q]
        rows = piece(zh_, h, u)
        for d in range(2):
            arrived(got2.at[d, rows, :], share_number("S3" if h == d else "S2", zh_, u, d))
        return p_buf[3, rows, :] + got2[0, rows, :].astype(F32) + got2[1, rows, :].astype(F32)

    def send_z(u):
        for h in range(2):
            z_send[u, h * PIECE : (h + 1) * PIECE, :] = summed(0, u, h).astype(BF16)
        send(z_send.at[u], z_got.at[u], number("Z", u), device(zh_=other))

    def own_sums(u):
        for h in range(2):
            p_buf[0, h * TOK + u * PIECE : h * TOK + (u + 1) * PIECE, :] = summed(1, u, h)

    def a_rest():
        arrived(a_block(x, zh, 1 - k), number("AS"))
        for d in range(2):
            arrived(a_block(x_at[1 - d], zh, 1 - d), number("AX", 2 * d + 1 - d))
            arrived(a_block(wrap(x + 2), zh, d), number("AF", d))
            arrived(a_block(x_at[1 - d], other, 1 - d), number("AP", 2 * d + 1 - d))
            arrived(a_block(wrap(x + 2), other, d), number("APF", d))

    def factors():
        turn(a_buf, at_buf, 0, TOKENS // TOK)
        factor_grads(at_buf, g_buf, mask_buf, r_buf, l_buf, lpart, rpart)
        for i in range(2):
            lx[x, :, i * (HALF // 2) : (i + 1) * (HALF // 2)] = lpart[i]
        send(rpart.at[:, sib_cols], rgot, number("RC"), sibling)
        for i in range(1, 4):
            send(lx.at[x], lx.at[x], number("LX", i - 1), device(x_=wrap(x + i)))

    def factors_y():
        arrived(rgot, number("RC"))
        ry[y] = rpart[:, :COLS] + rgot[...]
        for i in range(1, 4):
            send(ry.at[y], ry.at[y], number("RY", i - 1), device(y_=wrap(y + i)))

    def factors_x():
        for i in range(1, 4):
            arrived(lx.at[wrap(x + 4 - i)], number("LX", i - 1))
        lz[...] = (lx[0] + lx[1]) + (lx[2] + lx[3])
        for i, to in enumerate((device(zh_=other), sibling, device(zh_=other, k_=1 - k))):
            send(lz, lgot.at[i], number("LZ", i), to)

    def factors_z():
        for i in range(1, 4):
            arrived(ry.at[wrap(y + 4 - i)], number("RY", i - 1))
        rz[zl] = (ry[0] + ry[1]) + (ry[2] + ry[3])
        for i in range(1, 4):
            send(rz.at[zl], rz.at[zl], number("RZ", i - 1), device(zl_=wrap(zl + i)))

    def factors_end():
        for i in range(3):
            arrived(lgot.at[i], number("LZ", i))
        left_out[:, half(k)] = lz[...] + lgot[0]
        left_out[:, half(1 - k)] = lgot[1] + lgot[2]
        for i in range(1, 4):
            arrived(rz.at[wrap(zl + 4 - i)], number("RZ", i - 1))
        right_out[...] = (rz[0] + rz[1]) + (rz[2] + rz[3])

    zs = (other, zh)

    send_a_x()
    send_g()
    send_sibling()
    merge_own()
    g_from_y(0)
    g_from_z(1)
    g_from_z(3)
    a_forward("AF", "AX", zh, 0)
    a_forward("AF", "AX", zh, 1)
    g_from_z(2)
    send_a_z(0)
    merge_sibling()
    g_from_y(1)
    g_from_y(3)
    g_from_far(0)
    g_from_y(2)
    g_from_far(1)
    g_from_far(3)
    g_from_far(2)
    sent(number("AZ"))
    send_a_z(1)
    a_from_z(0)
    g_all()

    product(0, wrap(x + 2), g_buf, m_buf, p_buf)
    for u in range(2):
        send_far(0, u)
    for d in range(2):
        product(1 + d, x_at[d], g_buf, m_buf, p_buf)
        for u in range(2):
            send_near(0, u, d)
    product(3, x, g_buf, m_buf, p_buf)
    a_from_z(1)
    for u in range(2):
        send_far(1, u)
    for u in range(2):
        pass_on(0, u)
    a_forward("APF", "AP", other, 0)
    a_forward("APF", "AP", other, 1)
    for u in range(2):
        for d in range(2):
            send_near(1, u, d)
    send_z(0)
    pass_on(1, 0)
    send_z(1)
    pass_on(1, 1)
    a_rest()
    factors()
    factors_y()
    factors_x()
    factors_z()
    factors_end()

    for u in range(2):
        own_sums(u)
    theirs = pl.multiple_of((1 - k) * TOK, TOK)
    ours = pl.multiple_of(k * TOK, TOK)
    for u in range(2):
        arrived(z_got.at[u], number("Z", u))
        part = slice(u * PIECE, (u + 1) * PIECE)

        def total(first, h):
            sums = p_buf[0, pl.ds(first + u * PIECE, PIECE), :]
            return (sums + z_got[u, pl.ds(pl.multiple_of(h * PIECE, PIECE), PIECE), :].astype(F32)).astype(BF16)

        o_send[part, :] = total(theirs, 1 - k)
        send(o_send.at[part, :], out.at[part, half(k)], number("O", u), sibling)
        o_own[part, :] = total(ours, k)
        pltpu.make_async_copy(o_own.at[part, :], out.at[part, half(k)], local_sem.at[u]).start()
    for u in range(2):
        part = slice(u * PIECE, (u + 1) * PIECE)
        pltpu.make_async_copy(o_own.at[part, :], out.at[part, half(k)], local_sem.at[u]).wait()
        arrived(out.at[part, half(1 - k)], number("O", u))
    for copy in pending.values():
        copy.wait_send()


def place(*arrays):
    def move(*refs):
        for src, dst in zip(refs[:3], refs[3:]):
            dst[...] = src[...]

    return pl.pallas_call(
        move,
        out_shape=tuple(jax.ShapeDtypeStruct(v.shape, v.dtype) for v in arrays),
        name="place_results",
    )(*arrays)


def per_device(a, g, w, code, lf, rf):
    anywhere = pl.BlockSpec(memory_space=pl.ANY)
    vmem = pl.BlockSpec(memory_space=pltpu.VMEM)
    out, left, right = pl.pallas_call(
        kernel,
        out_shape=(
            jax.ShapeDtypeStruct((TOK, HID), BF16),
            jax.ShapeDtypeStruct((RANK, HID), F32),
            jax.ShapeDtypeStruct((RANK, COLS), F32),
        ),
        in_specs=[anywhere] * 6,
        out_specs=(anywhere, vmem, vmem),
        scratch_shapes=[
            pltpu.VMEM((TOKENS, HALF), BF16),
            pltpu.VMEM((HALF, TOKENS), BF16),
            pltpu.VMEM((TOKENS, BOTH), BF16),
            pltpu.VMEM((HALF, BOTH), BF16),
            pltpu.VMEM((HALF // 4, BOTH), jnp.int32),
            pltpu.VMEM((RANK, BOTH), BF16),
            pltpu.VMEM((RANK, HALF), BF16),
            pltpu.VMEM((HALF, BOTH), BF16),
            pltpu.VMEM((HALF, BOTH), BF16),
            pltpu.VMEM((4, 4 * TOK, HALF), F32),
            pltpu.VMEM((3, 4 * TOK, HALF), BF16),
            pltpu.VMEM((2, 4 * TOK, HALF), BF16),
            pltpu.VMEM((2, 4 * TOK, HALF), BF16),
            pltpu.VMEM((2, TOK, HALF), BF16),
            pltpu.VMEM((2, TOK, HALF), BF16),
            pltpu.VMEM((TOK, HALF), BF16),
            pltpu.VMEM((TOK, HALF), BF16),
            pltpu.VMEM((2, RANK, HALF // 2), F32),
            pltpu.VMEM((4, RANK, HALF), F32),
            pltpu.VMEM((RANK, HALF), F32),
            pltpu.VMEM((3, RANK, HALF), F32),
            pltpu.VMEM((RANK, BOTH), F32),
            pltpu.VMEM((RANK, COLS), F32),
            pltpu.VMEM((4, RANK, COLS), F32),
            pltpu.VMEM((4, RANK, COLS), F32),
            pltpu.SemaphoreType.DMA((COPIES,)),
            pltpu.SemaphoreType.DMA((COPIES,)),
            pltpu.SemaphoreType.DMA((6,)),
        ],
        compiler_params=pltpu.CompilerParams(
            collective_id=0, has_side_effects=True, vmem_limit_bytes=58 << 20
        ),
        cost_estimate=pl.CostEstimate(flops=7_600_000_000, bytes_accessed=5_000_000, transcendentals=0),
        name="down_projection_backward",
    )(a, g, w, code, lf.T, rf)
    out, left, right = place(out, left, right)
    return out, left.T, right


def solution(mesh):
    in_specs = (
        P("col", "row"),
        P("row", "col"),
        P("row", "col"),
        P("row", "col"),
        P("row", None),
        P(None, "col"),
    )
    out_specs = (P("col", "row"), P("row", None), P(None, "col"))
    return jax.shard_map(
        per_device, mesh=mesh, in_specs=in_specs, out_specs=out_specs, check_vma=False
    )
```

```python
import functools

import jax
import jax.numpy as jnp
from jax import lax
from jax.experimental import pallas as pl
from jax.experimental.pallas import tpu as pltpu
from jax.sharding import PartitionSpec as P

MESH = pl.DeviceIdType.MESH
BF16, F32 = jnp.bfloat16, jnp.float32
TOKENS, RANK = 2048, 16
TOK, HID, COLS = 128, 1792, 512
HALF, BOTH = HID // 2, 2 * COLS
NT = (((1,), (1,)), ((), ()))
TN = (((0,), (0,)), ((), ()))
HT = 128
PIECE = TOK // 2
LROWS, RCOLS = RANK // 4, COLS // 4
WIDE = ((0, 256), (256, 256), (512, 256), (768, 128))

NUMBERS = {}


def numbered(name, count):
    NUMBERS[name] = sum(c for _, c in NUMBERS.values()), count


for _name, _count in (
    ("AX", 4), ("AZ", 2), ("AS", 1), ("AF", 2), ("AP", 4), ("APF", 2),
    ("GZ", 3), ("GY", 8), ("GF", 4), ("GS", 16),
    ("W", 1), ("C", 1), ("R", 1),
    ("S1", 8), ("S2", 8), ("S3", 8), ("Z", 2), ("O", 2),
    ("LX", 3), ("LZ", 1), ("LG", 7), ("RC", 1), ("RY", 3), ("RZ", 3), ("RG", 3),
):
    numbered(_name, _count)
COPIES = sum(c for _, c in NUMBERS.values())


def number(name, index=0):
    return NUMBERS[name][0] + index


def merge_tiles(slot, w_buf, c_buf, r_buf, l_buf, mask_buf, m_buf):
    cols = pl.ds(slot * COLS, COLS)
    groups = HT // 4
    row = lax.broadcasted_iota(jnp.int32, (HT, HT), 0)
    lane = lax.broadcasted_iota(jnp.int32, (HT, HT), 1)
    hit = (row % 4 == lane // groups) & (row // 4 == lane % groups)
    spread = jnp.where(hit, 1.0, 0.0).astype(BF16)
    right = r_buf[:, cols]

    def tile(i, _):
        code = c_buf[pl.ds(pl.multiple_of(i * groups, groups), groups), cols]
        is0, is1, is2 = code == 0, code == 1, code == 2
        is3, is4, is5 = code == 3, code == 4, code == 5
        kept = (is0 | is1 | is2, is0 | is3 | is4, is1 | is3 | is5, is2 | is4 | is5)
        kept = jnp.concatenate([jnp.where(b, 1.0, 0.0) for b in kept], axis=0).astype(BF16)
        mask = jnp.dot(spread, kept, preferred_element_type=F32)
        rows = pl.ds(pl.multiple_of(i * HT, HT), HT)
        low = lax.dot_general(l_buf[:, rows], right, TN, preferred_element_type=F32)
        merged = mask * (w_buf[rows, cols].astype(F32) + 2.0 * low)
        mask_buf[rows, cols] = mask.astype(BF16)
        m_buf[rows, cols] = merged.astype(BF16)
        return 0

    lax.fori_loop(0, HALF // HT, tile, 0)


def product(i, x_dest, g_buf, m_buf, p_buf):
    first = pl.multiple_of(x_dest * 4 * TOK, 4 * TOK)
    for at, size in WIDE:
        p_buf[i, :, at : at + size] = lax.dot_general(
            g_buf[pl.ds(first, 4 * TOK), :], m_buf[at : at + size, :], NT, preferred_element_type=F32
        )


def turn(a_buf, at_buf, zh):
    def block(i, _):
        toks = pl.ds(pl.multiple_of(((i // 2) * 4 + zh * 2 + i % 2) * TOK, TOK), TOK)
        at_buf[:, toks] = a_buf[toks, :].T
        return 0

    lax.fori_loop(0, TOKENS // TOK // 2, block, 0)


def factor_grads(first, last, at_buf, g_buf, mask_buf, r_buf, l_buf, left, right):
    if first == 0:
        left[...] = jnp.zeros_like(left)
    step = 512

    def tile(n, _):
        cols = pl.ds(pl.multiple_of(n * step, step), step)
        total = jnp.zeros((RANK, step), F32)
        for half in range(2):
            rows = pl.ds(half * (HALF // 2), HALF // 2)
            grad = jnp.dot(at_buf[rows, :], g_buf[:, cols], preferred_element_type=F32)
            pruned = (mask_buf[rows, cols].astype(F32) * grad * (1.0 / TOKENS)).astype(BF16)
            total += jnp.dot(l_buf[:, rows], pruned, preferred_element_type=F32)
            left[half] += 2.0 * lax.dot_general(
                r_buf[:, cols], pruned, NT, preferred_element_type=F32
            )
        right[:, cols] = 2.0 * total
        return 0

    lax.fori_loop(first, last, tile, 0)


def kernel(
    a, g, w, code, lf, rf, out, left_out, right_out,
    a_buf, at_buf, g_buf, w_buf, c_buf, r_buf, l_buf, mask_buf, m_buf,
    p_buf, s_buf, got1, got2, z_send, z_got, o_send, o_own,
    lpart, lx_send, lx, lz, lz_got, lall, rpart, rgot, ry_send, ry, rz, rall,
    send_sem, recv_sem, local_sem,
):
    row, col = lax.axis_index("row"), lax.axis_index("col")
    y, zl = row // 4, row % 4
    x, zh, k = col // 4, (col // 2) % 2, col % 2
    other = 1 - zh

    def device(y_=y, zl_=zl, x_=x, zh_=zh, k_=k):
        return (y_ * 4 + zl_, x_ * 4 + zh_ * 2 + k_)

    def wrap(v):
        return v % 4

    x_at = (wrap(x + 1), wrap(x + 3))
    y_at = (wrap(y + 1), wrap(y + 3))
    sibling = device(k_=1 - k)
    peers = [sibling]
    peers += [device(x_=x_at[d], k_=j) for d in range(2) for j in range(2)]
    peers += [device(x_=wrap(x + 2), k_=j) for j in range(2)]
    peers += [device(zh_=other, k_=j) for j in range(2)]
    peers += [device(y_=wrap(y + i)) for i in range(1, 4)]
    peers += [device(zl_=wrap(zl + i)) for i in range(1, 4)]

    pending = {}

    def send(src, dst, n, to, recv_n=None, keep=True):
        copy = pltpu.make_async_remote_copy(
            src_ref=src, dst_ref=dst, send_sem=send_sem.at[n],
            recv_sem=recv_sem.at[n if recv_n is None else recv_n],
            device_id=to, device_id_type=MESH,
        )
        copy.start()
        if keep:
            pending[n] = copy

    def arrived(dst, n):
        pltpu.make_async_remote_copy(
            src_ref=dst, dst_ref=dst, send_sem=send_sem.at[n], recv_sem=recv_sem.at[n],
            device_id=sibling, device_id_type=MESH,
        ).wait_recv()

    def left(src, n):
        pltpu.make_async_remote_copy(
            src_ref=src, dst_ref=src, send_sem=send_sem.at[n], recv_sem=recv_sem.at[n],
            device_id=sibling, device_id_type=MESH,
        ).wait_send()

    def sent(n):
        pending.pop(n).wait_send()

    def tokens_of(x_, zh_, k_):
        return pl.ds(pl.multiple_of((x_ * 4 + zh_ * 2 + k_) * TOK, TOK), TOK)

    def a_block(x_, zh_, k_):
        return a_buf.at[tokens_of(x_, zh_, k_), :]

    def g_block(y_, zl_, slot=0):
        return g_buf.at[pl.ds(pl.multiple_of((y_ * 4 + zl_) * TOK, TOK), TOK), pl.ds(slot * COLS, COLS)]

    def half(j):
        return pl.ds(pl.multiple_of(j * HALF, HALF), HALF)

    def quarter(j):
        return pl.ds(pl.multiple_of(j * (HALF // 4), HALF // 4), HALF // 4)

    own_cols, sib_cols = pl.ds(0, COLS), pl.ds(COLS, COLS)

    locals_ = [
        pltpu.make_async_copy(src, dst, local_sem.at[n])
        for n, (src, dst) in enumerate((
            (w.at[half(k), :], w_buf.at[:, own_cols]),
            (code.at[quarter(k), :], c_buf.at[:, own_cols]),
            (lf.at[:, half(k)], l_buf),
            (rf, r_buf.at[:, own_cols]),
            (a.at[:, half(k)], a_block(x, zh, k)),
            (g, g_block(y, zl)),
        ))
    ]
    for copy in locals_:
        copy.start()

    barrier = pltpu.get_barrier_semaphore()
    for peer in peers:
        pl.semaphore_signal(barrier, inc=1, device_id=peer, device_id_type=MESH)
    pl.semaphore_wait(barrier, len(peers))

    def send_a_x():
        for j in range(2):
            for d in range(2):
                send(a.at[:, half(j)], a_block(x, zh, k), number("AX", 2 * d + j), device(x_=x_at[d], k_=j),
                     number("AX", 2 * d) + k)

    def send_g():
        for d in range(2):
            send(g, g_block(y, zl), number("GY", 4 * d), device(y_=y_at[d]))
        for i in (1, 3, 2):
            send(g, g_block(y, zl), number("GZ", i - 1), device(zl_=wrap(zl + i)))

    def send_a_z(i):
        j = k if i == 0 else 1 - k
        send(a.at[:, half(j)], a_block(x, zh, k), number("AZ", i), device(zh_=other, k_=j), number("AZ") + k)

    def send_sibling():
        send(g, g_block(y, zl, 1), number("GS"), sibling)
        send(rf, r_buf.at[:, sib_cols], number("R"), sibling)
        send(code.at[quarter(1 - k), :], c_buf.at[:, sib_cols], number("C"), sibling)
        send(w.at[half(1 - k), :], w_buf.at[:, sib_cols], number("W"), sibling)
        send(a.at[:, half(1 - k)], a_block(x, zh, k), number("AS"), sibling)

    def merge_own():
        for copy in locals_:
            copy.wait()
        merge_tiles(0, w_buf, c_buf, r_buf, l_buf, mask_buf, m_buf)

    def merge_sibling():
        for name, ref in (("R", r_buf), ("C", c_buf), ("W", w_buf)):
            arrived(ref.at[:, sib_cols], number(name))
        merge_tiles(1, w_buf, c_buf, r_buf, l_buf, mask_buf, m_buf)

    def g_to_sibling(n, y_, zl_):
        send(g_block(y_, zl_), g_block(y_, zl_, 1), number("GS", n), sibling)

    def a_forward(name, base, zh_, d):
        block = a_block(x_at[1 - d], zh_, d)
        arrived(block, number(base, 2 * d + d))
        send(block, block, number(name, d), device(x_=x_at[d]))

    def a_from_z(i):
        o = k if i == 0 else 1 - k
        block = a_block(x, other, o)
        arrived(block, number("AZ") + o)
        for d in range(2):
            send(block, block, number("AP", 2 * d + i), device(x_=x_at[d]), number("AP", 2 * d) + o)

    def g_from_z(i):
        block = g_block(y, wrap(zl + 4 - i))
        arrived(block, number("GZ", i - 1))
        for d in range(2):
            send(block, block, number("GY", 4 * d + i), device(y_=y_at[d]))
        g_to_sibling(i, y, wrap(zl + 4 - i))

    def g_from_y(i):
        for d in (i % 2, 1 - i % 2):
            from_y, from_zl = y_at[1 - d], wrap(zl + 4 - i)
            block = g_block(from_y, from_zl)
            arrived(block, number("GY", 4 * d + i))
            if i % 2 == d:
                send(block, block, number("GF", i), device(y_=y_at[d]))
            g_to_sibling(4 + 4 * d + i, from_y, from_zl)

    def g_from_far(i):
        block = g_block(wrap(y + 2), wrap(zl + 4 - i))
        arrived(block, number("GF", i))
        g_to_sibling(12 + i, wrap(y + 2), wrap(zl + 4 - i))

    def g_row(e):
        first = {0: 0, 3: 4, 1: 8, 2: 12}[e]
        for i in range(4):
            arrived(g_block(wrap(y + e), wrap(zl + 4 - i), 1), number("GS", first + i))

    def piece(zh_, h, u):
        return pl.ds(pl.multiple_of(zh_ * 2 * TOK + h * TOK + u * PIECE, PIECE), PIECE)

    def share_number(name, zh_, u, d):
        return number(name) + (zh_ * 4 + u * 2 + d)

    def send_far(q, u):
        zh_ = zs[q]
        for d in range(2):
            rows = piece(zh_, d, u)
            s_buf[2, rows, :] = p_buf[2, rows, :].astype(BF16)
            send(s_buf.at[2, rows, :], got1.at[d, rows, :], number("S1", 4 * q + 2 * u + d),
                 device(x_=x_at[d]), share_number("S1", zh_, u, d), keep=False)

    def send_near(q, u, d):
        zh_ = zs[q]
        rows = piece(zh_, 1 - d, u)
        to = 1 + 2 * d
        s_buf[to, rows, :] = p_buf[to, rows, :].astype(BF16)
        send(s_buf.at[to, rows, :], got2.at[d, rows, :], number("S2", 4 * q + 2 * u + d),
             device(x_=x_at[d]), share_number("S2", zh_, u, d), keep=False)

    def shares(e):
        g_row(e)
        place_ = wrap(y + e + 4 - x)
        product(place_, wrap(y + e), g_buf, m_buf, p_buf)
        early = (0, 1) if e == 0 else (0,)

        @pl.when(place_ == 2)
        def _():
            for q in early:
                for u in range(2):
                    send_far(q, u)

        for d in range(2):

            @pl.when(place_ == 1 + 2 * d)
            def _():
                for q in early:
                    for u in range(2):
                        send_near(q, u, d)

    def shares_later():
        place_ = wrap(y + 4 - x)

        @pl.when(place_ != 2)
        def _():
            for u in range(2):
                send_far(1, u)

        for d in range(2):

            @pl.when(place_ != 1 + 2 * d)
            def _():
                for u in range(2):
                    send_near(1, u, d)

    def pass_on(q, u):
        zh_ = zs[q]
        for d in range(2):
            rows = piece(zh_, d, u)
            arrived(got1.at[d, rows, :], share_number("S1", zh_, u, d))
            to = 1 + 2 * d
            s_buf[to, rows, :] = (p_buf[to, rows, :] + got1[d, rows, :].astype(F32)).astype(BF16)
            send(s_buf.at[to, rows, :], got2.at[d, rows, :], number("S3", 4 * q + 2 * u + d),
                 device(x_=x_at[d]), share_number("S3", zh_, u, d))

    def summed(q, u, h):
        zh_ = zs[q]
        rows = piece(zh_, h, u)
        for d in range(2):
            arrived(got2.at[d, rows, :], share_number("S3" if h == d else "S2", zh_, u, d))
        return p_buf[0, rows, :] + got2[0, rows, :].astype(F32) + got2[1, rows, :].astype(F32)

    def send_z(u):
        for h in range(2):
            z_send[u, h * PIECE : (h + 1) * PIECE, :] = summed(0, u, h).astype(BF16)
        send(z_send.at[u], z_got.at[u], number("Z", u), device(zh_=other))

    def own_sums(u):
        for h in range(2):
            p_buf[2, h * TOK + u * PIECE : h * TOK + (u + 1) * PIECE, :] = summed(1, u, h)

    def a_rest(zh_, near, far):
        for d in range(2):
            arrived(a_block(x_at[1 - d], zh_, 1 - d), number(near, 2 * d + 1 - d))
            arrived(a_block(wrap(x + 2), zh_, d), number(far, d))
        turn(a_buf, at_buf, zh_)

    def factors(first, last):
        factor_grads(first, last, at_buf, g_buf, mask_buf, r_buf, l_buf, lpart, rpart)

    def factors_send():
        send(rpart.at[:, sib_cols], rgot, number("RC"), sibling)
        for q in range(4):
            rows = slice(q * LROWS, (q + 1) * LROWS)
            lx_send[q] = jnp.concatenate([lpart[0, rows, :], lpart[1, rows, :]], axis=1)
        lx[x] = lx_send[x]
        for i in range(1, 4):
            send(lx_send.at[wrap(x + i)], lx.at[x], number("LX", i - 1), device(x_=wrap(x + i)))

    def factors_y():
        arrived(rgot, number("RC"))
        for q in range(4):
            lanes = slice(q * RCOLS, (q + 1) * RCOLS)
            ry_send[q] = rpart[:, lanes] + rgot[:, lanes]
        ry[y] = ry_send[y]
        for i in range(1, 4):
            send(ry_send.at[wrap(y + i)], ry.at[y], number("RY", i - 1), device(y_=wrap(y + i)))

    def factors_x():
        for i in range(1, 4):
            arrived(lx.at[wrap(x + 4 - i)], number("LX", i - 1))
        lz[...] = (lx[0] + lx[1]) + (lx[2] + lx[3])
        send(lz, lz_got, number("LZ"), device(zh_=other))

    def factors_z():
        for i in range(1, 4):
            arrived(ry.at[wrap(y + 4 - i)], number("RY", i - 1))
        rz[zl] = (ry[0] + ry[1]) + (ry[2] + ry[3])
        for i in range(1, 4):
            send(rz.at[zl], rz.at[zl], number("RZ", i - 1), device(zl_=wrap(zl + i)))

    def left_share():
        arrived(lz_got, number("LZ"))
        lall[k, x] = lz[...] + lz_got[...]
        for i in range(4):
            for c in range(2):
                if i or c:
                    send(lall.at[k, x], lall.at[k, x], number("LG", 2 * i + c - 1),
                         device(x_=wrap(x + i), k_=k if c == 0 else 1 - k))

    def right_share():
        for i in range(1, 4):
            arrived(rz.at[wrap(zl + 4 - i)], number("RZ", i - 1))
        rall[y] = (rz[0] + rz[1]) + (rz[2] + rz[3])
        for i in range(1, 4):
            send(rall.at[y], rall.at[y], number("RG", i - 1), device(y_=wrap(y + i)))

    def factors_end():
        for i in range(4):
            for c in range(2):
                if i or c:
                    arrived(lall.at[k if c == 0 else 1 - k, wrap(x + 4 - i)], number("LG", 2 * i + c - 1))
        for c in range(2):
            for q in range(4):
                left_out[q * LROWS : (q + 1) * LROWS, c * HALF : (c + 1) * HALF] = lall[c, q]
        for i in range(1, 4):
            arrived(rall.at[wrap(y + 4 - i)], number("RG", i - 1))
        for q in range(4):
            right_out[:, q * RCOLS : (q + 1) * RCOLS] = rall[q]

    zs = (other, zh)

    send_a_x()
    send_g()
    send_sibling()
    merge_own()
    g_from_y(0)
    g_from_z(1)
    g_from_z(3)
    a_forward("AF", "AX", zh, 0)
    a_forward("AF", "AX", zh, 1)
    g_from_z(2)
    send_a_z(0)
    merge_sibling()
    shares(0)
    g_from_y(1)
    g_from_y(3)
    g_from_far(0)
    g_from_y(2)
    g_from_far(1)
    shares(3)
    shares(1)
    g_from_far(3)
    g_from_far(2)
    sent(number("AZ"))
    send_a_z(1)
    a_from_z(0)
    shares(2)
    arrived(a_block(x, zh, 1 - k), number("AS"))
    a_rest(zh, "AX", "AF")
    a_from_z(1)
    pass_on(0, 0)
    pass_on(0, 1)
    a_forward("APF", "AP", other, 0)
    a_forward("APF", "AP", other, 1)
    send_z(0)
    shares_later()
    send_z(1)
    a_rest(other, "AP", "APF")
    factors(0, 1)
    pass_on(1, 0)
    pass_on(1, 1)
    factors(1, 2)
    factors_send()
    factors_y()
    factors_x()
    factors_z()
    left_share()
    right_share()

    for u in range(2):
        own_sums(u)
    factors_end()
    theirs = pl.multiple_of((1 - k) * TOK, TOK)
    ours = pl.multiple_of(k * TOK, TOK)
    for u in range(2):
        arrived(z_got.at[u], number("Z", u))
        part = slice(u * PIECE, (u + 1) * PIECE)

        def total(first, h):
            sums = p_buf[2, pl.ds(first + u * PIECE, PIECE), :]
            return (sums + z_got[u, pl.ds(pl.multiple_of(h * PIECE, PIECE), PIECE), :].astype(F32)).astype(BF16)

        o_send[part, :] = total(theirs, 1 - k)
        send(o_send.at[part, :], out.at[part, half(k)], number("O", u), sibling)
        o_own[part, :] = total(ours, k)
        pltpu.make_async_copy(o_own.at[part, :], out.at[part, half(k)], local_sem.at[u]).start()
    for u in range(2):
        part = slice(u * PIECE, (u + 1) * PIECE)
        pltpu.make_async_copy(o_own.at[part, :], out.at[part, half(k)], local_sem.at[u]).wait()
        arrived(out.at[part, half(1 - k)], number("O", u))
    for copy in pending.values():
        copy.wait_send()
    for n in range(8):
        for name in ("S1", "S2"):
            left(s_buf.at[0, pl.ds(0, PIECE), :], number(name, n))


def place(*arrays):
    def move(*refs):
        for src, dst in zip(refs[:3], refs[3:]):
            dst[...] = src[...]

    return pl.pallas_call(
        move,
        out_shape=tuple(jax.ShapeDtypeStruct(v.shape, v.dtype) for v in arrays),
        name="place_results",
    )(*arrays)


def per_device(a, g, w, code, lf, rf):
    anywhere = pl.BlockSpec(memory_space=pl.ANY)
    vmem = pl.BlockSpec(memory_space=pltpu.VMEM)
    out, left, right = pl.pallas_call(
        kernel,
        out_shape=(
            jax.ShapeDtypeStruct((TOK, HID), BF16),
            jax.ShapeDtypeStruct((RANK, HID), F32),
            jax.ShapeDtypeStruct((RANK, COLS), F32),
        ),
        in_specs=[anywhere] * 6,
        out_specs=(anywhere, vmem, vmem),
        scratch_shapes=[
            pltpu.VMEM((TOKENS, HALF), BF16),
            pltpu.VMEM((HALF, TOKENS), BF16),
            pltpu.VMEM((TOKENS, BOTH), BF16),
            pltpu.VMEM((HALF, BOTH), BF16),
            pltpu.VMEM((HALF // 4, BOTH), jnp.int32),
            pltpu.VMEM((RANK, BOTH), BF16),
            pltpu.VMEM((RANK, HALF), BF16),
            pltpu.VMEM((HALF, BOTH), BF16),
            pltpu.VMEM((HALF, BOTH), BF16),
            pltpu.VMEM((4, 4 * TOK, HALF), F32),
            pltpu.VMEM((4, 4 * TOK, HALF), BF16),
            pltpu.VMEM((2, 4 * TOK, HALF), BF16),
            pltpu.VMEM((2, 4 * TOK, HALF), BF16),
            pltpu.VMEM((2, TOK, HALF), BF16),
            pltpu.VMEM((2, TOK, HALF), BF16),
            pltpu.VMEM((TOK, HALF), BF16),
            pltpu.VMEM((TOK, HALF), BF16),
            pltpu.VMEM((2, RANK, HALF // 2), F32),
            pltpu.VMEM((4, LROWS, HALF), F32),
            pltpu.VMEM((4, LROWS, HALF), F32),
            pltpu.VMEM((LROWS, HALF), F32),
            pltpu.VMEM((LROWS, HALF), F32),
            pltpu.VMEM((2, 4, LROWS, HALF), F32),
            pltpu.VMEM((RANK, BOTH), F32),
            pltpu.VMEM((RANK, COLS), F32),
            pltpu.VMEM((4, RANK, RCOLS), F32),
            pltpu.VMEM((4, RANK, RCOLS), F32),
            pltpu.VMEM((4, RANK, RCOLS), F32),
            pltpu.VMEM((4, RANK, RCOLS), F32),
            pltpu.SemaphoreType.DMA((COPIES,)),
            pltpu.SemaphoreType.DMA((COPIES,)),
            pltpu.SemaphoreType.DMA((6,)),
        ],
        compiler_params=pltpu.CompilerParams(
            collective_id=0, has_side_effects=True, vmem_limit_bytes=58 << 20
        ),
        cost_estimate=pl.CostEstimate(flops=7_600_000_000, bytes_accessed=5_000_000, transcendentals=0),
        name="down_projection_backward",
    )(a, g, w, code, lf.T, rf)
    out, left, right = place(out, left, right)
    return out, left.T, right


def solution(mesh):
    in_specs = (
        P("col", "row"),
        P("row", "col"),
        P("row", "col"),
        P("row", "col"),
        P("row", None),
        P(None, "col"),
    )
    out_specs = (P("col", "row"), P("row", None), P(None, "col"))
    return jax.shard_map(
        per_device, mesh=mesh, in_specs=in_specs, out_specs=out_specs, check_vma=False
    )
```

```python
import functools

import jax
import jax.numpy as jnp
from jax import lax
from jax.experimental import pallas as pl
from jax.experimental.pallas import tpu as pltpu
from jax.sharding import PartitionSpec as P

MESH = pl.DeviceIdType.MESH
BF16, F32 = jnp.bfloat16, jnp.float32
TOKENS, RANK = 2048, 16
TOK, HID, COLS = 128, 1792, 512
HALF, BOTH = HID // 2, 2 * COLS
NT = (((1,), (1,)), ((), ()))
TN = (((0,), (0,)), ((), ()))
HT = 128
PIECE = TOK // 2
LROWS, RCOLS = RANK // 4, COLS // 4
WIDE = ((0, 256), (256, 256), (512, 256), (768, 128))

NUMBERS = {}


def numbered(name, count):
    NUMBERS[name] = sum(c for _, c in NUMBERS.values()), count


for _name, _count in (
    ("AX", 4), ("AZ", 2), ("AS", 1), ("AF", 2), ("AP", 4), ("APF", 2),
    ("GZ", 3), ("GY", 8), ("GF", 4), ("GS", 16),
    ("W", 1), ("C", 1), ("R", 1),
    ("S1", 8), ("S2", 8), ("S3", 8), ("Z", 2), ("O", 2),
    ("LX", 3), ("LZ", 1), ("LG", 7), ("RC", 1), ("RY", 3), ("RZ", 3), ("RG", 3),
):
    numbered(_name, _count)
COPIES = sum(c for _, c in NUMBERS.values())


def number(name, index=0):
    return NUMBERS[name][0] + index


def merge_tiles(slot, w_buf, c_buf, r_buf, l_buf, mask_buf, m_buf):
    cols = pl.ds(slot * COLS, COLS)
    groups = HT // 4
    row = lax.broadcasted_iota(jnp.int32, (HT, HT), 0)
    lane = lax.broadcasted_iota(jnp.int32, (HT, HT), 1)
    hit = (row % 4 == lane // groups) & (row // 4 == lane % groups)
    spread = jnp.where(hit, 1.0, 0.0).astype(BF16)
    right = r_buf[:, cols]

    def tile(i, _):
        code = c_buf[pl.ds(pl.multiple_of(i * groups, groups), groups), cols]
        is0, is1, is2 = code == 0, code == 1, code == 2
        is3, is4, is5 = code == 3, code == 4, code == 5
        kept = (is0 | is1 | is2, is0 | is3 | is4, is1 | is3 | is5, is2 | is4 | is5)
        kept = jnp.concatenate([jnp.where(b, 1.0, 0.0) for b in kept], axis=0).astype(BF16)
        mask = jnp.dot(spread, kept, preferred_element_type=F32)
        rows = pl.ds(pl.multiple_of(i * HT, HT), HT)
        low = lax.dot_general(l_buf[:, rows], right, TN, preferred_element_type=F32)
        merged = mask * (w_buf[rows, cols].astype(F32) + 2.0 * low)
        mask_buf[rows, cols] = mask.astype(BF16)
        m_buf[rows, cols] = merged.astype(BF16)
        return 0

    lax.fori_loop(0, HALF // HT, tile, 0)


def product(i, x_dest, g_buf, m_buf, p_buf):
    first = pl.multiple_of(x_dest * 4 * TOK, 4 * TOK)
    for at, size in WIDE:
        p_buf[i, :, at : at + size] = lax.dot_general(
            g_buf[pl.ds(first, 4 * TOK), :], m_buf[at : at + size, :], NT, preferred_element_type=F32
        )


def turn(a_buf, at_buf, zh):
    def block(i, _):
        toks = pl.ds(pl.multiple_of(((i // 2) * 4 + zh * 2 + i % 2) * TOK, TOK), TOK)
        at_buf[:, toks] = a_buf[toks, :].T
        return 0

    lax.fori_loop(0, TOKENS // TOK // 2, block, 0)


def factor_grads(first, last, at_buf, g_buf, mask_buf, r_buf, l_buf, left, right):
    if first == 0:
        left[...] = jnp.zeros_like(left)
    step = 512

    def tile(n, _):
        cols = pl.ds(pl.multiple_of(n * step, step), step)
        total = jnp.zeros((RANK, step), F32)
        for half in range(2):
            rows = pl.ds(half * (HALF // 2), HALF // 2)
            grad = jnp.dot(at_buf[rows, :], g_buf[:, cols], preferred_element_type=F32)
            pruned = (mask_buf[rows, cols].astype(F32) * grad * (1.0 / TOKENS)).astype(BF16)
            total += jnp.dot(l_buf[:, rows], pruned, preferred_element_type=F32)
            left[half] += 2.0 * lax.dot_general(
                r_buf[:, cols], pruned, NT, preferred_element_type=F32
            )
        right[:, cols] = 2.0 * total
        return 0

    lax.fori_loop(first, last, tile, 0)


def kernel(
    a, g, w, code, lf, rf, out, left_out, right_out,
    a_buf, at_buf, g_buf, w_buf, c_buf, r_buf, l_buf, mask_buf, m_buf,
    p_buf, s_buf, got1, got2, z_send, z_got, o_send, o_own,
    lpart, lx_send, lx, lz, lz_got, lall, rpart, rgot, ry_send, ry, rz, rall,
    send_sem, recv_sem, local_sem,
):
    row, col = lax.axis_index("row"), lax.axis_index("col")
    y, zl = row // 4, row % 4
    x, zh, k = col // 4, (col // 2) % 2, col % 2
    other = 1 - zh

    def device(y_=y, zl_=zl, x_=x, zh_=zh, k_=k):
        return (y_ * 4 + zl_, x_ * 4 + zh_ * 2 + k_)

    def wrap(v):
        return v % 4

    x_at = (wrap(x + 1), wrap(x + 3))
    y_at = (wrap(y + 1), wrap(y + 3))
    sibling = device(k_=1 - k)
    peers = [sibling]
    peers += [device(x_=x_at[d], k_=j) for d in range(2) for j in range(2)]
    peers += [device(x_=wrap(x + 2), k_=j) for j in range(2)]
    peers += [device(zh_=other, k_=j) for j in range(2)]
    peers += [device(y_=wrap(y + i)) for i in range(1, 4)]
    peers += [device(zl_=wrap(zl + i)) for i in range(1, 4)]

    pending = {}

    def send(src, dst, n, to, recv_n=None, keep=True):
        copy = pltpu.make_async_remote_copy(
            src_ref=src, dst_ref=dst, send_sem=send_sem.at[n],
            recv_sem=recv_sem.at[n if recv_n is None else recv_n],
            device_id=to, device_id_type=MESH,
        )
        copy.start()
        if keep:
            pending[n] = copy

    def arrived(dst, n):
        pltpu.make_async_remote_copy(
            src_ref=dst, dst_ref=dst, send_sem=send_sem.at[n], recv_sem=recv_sem.at[n],
            device_id=sibling, device_id_type=MESH,
        ).wait_recv()

    def left(src, n):
        pltpu.make_async_remote_copy(
            src_ref=src, dst_ref=src, send_sem=send_sem.at[n], recv_sem=recv_sem.at[n],
            device_id=sibling, device_id_type=MESH,
        ).wait_send()

    def sent(n):
        pending.pop(n).wait_send()

    def tokens_of(x_, zh_, k_):
        return pl.ds(pl.multiple_of((x_ * 4 + zh_ * 2 + k_) * TOK, TOK), TOK)

    def a_block(x_, zh_, k_):
        return a_buf.at[tokens_of(x_, zh_, k_), :]

    def g_block(y_, zl_, slot=0):
        return g_buf.at[pl.ds(pl.multiple_of((y_ * 4 + zl_) * TOK, TOK), TOK), pl.ds(slot * COLS, COLS)]

    def half(j):
        return pl.ds(pl.multiple_of(j * HALF, HALF), HALF)

    def quarter(j):
        return pl.ds(pl.multiple_of(j * (HALF // 4), HALF // 4), HALF // 4)

    own_cols, sib_cols = pl.ds(0, COLS), pl.ds(COLS, COLS)

    locals_ = [
        pltpu.make_async_copy(src, dst, local_sem.at[n])
        for n, (src, dst) in enumerate((
            (w.at[half(k), :], w_buf.at[:, own_cols]),
            (code.at[quarter(k), :], c_buf.at[:, own_cols]),
            (lf.at[:, half(k)], l_buf),
            (rf, r_buf.at[:, own_cols]),
            (a.at[:, half(k)], a_block(x, zh, k)),
            (g, g_block(y, zl)),
        ))
    ]
    for copy in locals_:
        copy.start()

    barrier = pltpu.get_barrier_semaphore()
    for peer in peers:
        pl.semaphore_signal(barrier, inc=1, device_id=peer, device_id_type=MESH)
    pl.semaphore_wait(barrier, len(peers))

    def send_a_x():
        for j in range(2):
            for d in range(2):
                send(a.at[:, half(j)], a_block(x, zh, k), number("AX", 2 * d + j), device(x_=x_at[d], k_=j),
                     number("AX", 2 * d) + k)

    def send_g():
        for d in range(2):
            send(g, g_block(y, zl), number("GY", 4 * d), device(y_=y_at[d]))
        for i in (1, 3, 2):
            send(g, g_block(y, zl), number("GZ", i - 1), device(zl_=wrap(zl + i)))

    def send_a_z(i):
        j = k if i == 0 else 1 - k
        send(a.at[:, half(j)], a_block(x, zh, k), number("AZ", i), device(zh_=other, k_=j), number("AZ") + k)

    def send_sibling():
        send(g, g_block(y, zl, 1), number("GS"), sibling)
        send(rf, r_buf.at[:, sib_cols], number("R"), sibling)
        send(code.at[quarter(1 - k), :], c_buf.at[:, sib_cols], number("C"), sibling)
        send(w.at[half(1 - k), :], w_buf.at[:, sib_cols], number("W"), sibling)
        send(a.at[:, half(1 - k)], a_block(x, zh, k), number("AS"), sibling)

    def merge_own():
        for copy in locals_:
            copy.wait()
        merge_tiles(0, w_buf, c_buf, r_buf, l_buf, mask_buf, m_buf)

    def merge_sibling():
        for name, ref in (("R", r_buf), ("C", c_buf), ("W", w_buf)):
            arrived(ref.at[:, sib_cols], number(name))
        merge_tiles(1, w_buf, c_buf, r_buf, l_buf, mask_buf, m_buf)

    def g_to_sibling(n, y_, zl_):
        send(g_block(y_, zl_), g_block(y_, zl_, 1), number("GS", n), sibling)

    def a_forward(name, base, zh_, d):
        block = a_block(x_at[1 - d], zh_, d)
        arrived(block, number(base, 2 * d + d))
        send(block, block, number(name, d), device(x_=x_at[d]))

    def a_from_z(i):
        o = k if i == 0 else 1 - k
        block = a_block(x, other, o)
        arrived(block, number("AZ") + o)
        for d in range(2):
            send(block, block, number("AP", 2 * d + i), device(x_=x_at[d]), number("AP", 2 * d) + o)

    def g_from_z(i):
        block = g_block(y, wrap(zl + 4 - i))
        arrived(block, number("GZ", i - 1))
        for d in range(2):
            send(block, block, number("GY", 4 * d + i), device(y_=y_at[d]))
        g_to_sibling(i, y, wrap(zl + 4 - i))

    def g_from_y(i):
        for d in (i % 2, 1 - i % 2):
            from_y, from_zl = y_at[1 - d], wrap(zl + 4 - i)
            block = g_block(from_y, from_zl)
            arrived(block, number("GY", 4 * d + i))
            if i % 2 == d:
                send(block, block, number("GF", i), device(y_=y_at[d]))
            g_to_sibling(4 + 4 * d + i, from_y, from_zl)

    def g_from_far(i):
        block = g_block(wrap(y + 2), wrap(zl + 4 - i))
        arrived(block, number("GF", i))
        g_to_sibling(12 + i, wrap(y + 2), wrap(zl + 4 - i))

    def g_row(e):
        first = {0: 0, 3: 4, 1: 8, 2: 12}[e]
        for i in range(4):
            arrived(g_block(wrap(y + e), wrap(zl + 4 - i), 1), number("GS", first + i))

    def piece(zh_, h, u):
        return pl.ds(pl.multiple_of(zh_ * 2 * TOK + h * TOK + u * PIECE, PIECE), PIECE)

    def share_number(name, zh_, u, d):
        return number(name) + (zh_ * 4 + u * 2 + d)

    def send_far(q, u):
        zh_ = zs[q]
        for d in range(2):
            rows = piece(zh_, d, u)
            s_buf[2, rows, :] = p_buf[2, rows, :].astype(BF16)
            send(s_buf.at[2, rows, :], got1.at[d, rows, :], number("S1", 4 * q + 2 * u + d),
                 device(x_=x_at[d]), share_number("S1", zh_, u, d), keep=False)

    def send_near(q, u, d):
        zh_ = zs[q]
        rows = piece(zh_, 1 - d, u)
        to = 1 + 2 * d
        s_buf[to, rows, :] = p_buf[to, rows, :].astype(BF16)
        send(s_buf.at[to, rows, :], got2.at[d, rows, :], number("S2", 4 * q + 2 * u + d),
             device(x_=x_at[d]), share_number("S2", zh_, u, d), keep=False)

    def shares(e):
        g_row(e)
        place_ = wrap(y + e + 4 - x)
        product(place_, wrap(y + e), g_buf, m_buf, p_buf)
        early = (0, 1) if e == 0 else (0,)

        @pl.when(place_ == 2)
        def _():
            for q in early:
                for u in range(2):
                    send_far(q, u)

        for d in range(2):

            @pl.when(place_ == 1 + 2 * d)
            def _():
                for q in early:
                    for u in range(2):
                        send_near(q, u, d)

    def shares_later():
        place_ = wrap(y + 4 - x)

        @pl.when(place_ != 2)
        def _():
            for u in range(2):
                send_far(1, u)

        for d in range(2):

            @pl.when(place_ != 1 + 2 * d)
            def _():
                for u in range(2):
                    send_near(1, u, d)

    def pass_on(q, u):
        zh_ = zs[q]
        for d in range(2):
            rows = piece(zh_, d, u)
            arrived(got1.at[d, rows, :], share_number("S1", zh_, u, d))
            to = 1 + 2 * d
            s_buf[to, rows, :] = (p_buf[to, rows, :] + got1[d, rows, :].astype(F32)).astype(BF16)
            send(s_buf.at[to, rows, :], got2.at[d, rows, :], number("S3", 4 * q + 2 * u + d),
                 device(x_=x_at[d]), share_number("S3", zh_, u, d))

    def summed(q, u, h):
        zh_ = zs[q]
        rows = piece(zh_, h, u)
        for d in range(2):
            arrived(got2.at[d, rows, :], share_number("S3" if h == d else "S2", zh_, u, d))
        return p_buf[0, rows, :] + got2[0, rows, :].astype(F32) + got2[1, rows, :].astype(F32)

    def send_z(u):
        for h in range(2):
            z_send[u, h * PIECE : (h + 1) * PIECE, :] = summed(0, u, h).astype(BF16)
        send(z_send.at[u], z_got.at[u], number("Z", u), device(zh_=other))

    def own_sums(u):
        for h in range(2):
            p_buf[2, h * TOK + u * PIECE : h * TOK + (u + 1) * PIECE, :] = summed(1, u, h)

    def a_rest(zh_, near, far):
        for d in range(2):
            arrived(a_block(x_at[1 - d], zh_, 1 - d), number(near, 2 * d + 1 - d))
            arrived(a_block(wrap(x + 2), zh_, d), number(far, d))
        turn(a_buf, at_buf, zh_)

    def factors(first, last):
        factor_grads(first, last, at_buf, g_buf, mask_buf, r_buf, l_buf, lpart, rpart)

    def factors_send():
        send(rpart.at[:, sib_cols], rgot, number("RC"), sibling)
        for q in range(4):
            rows = slice(q * LROWS, (q + 1) * LROWS)
            lx_send[q] = jnp.concatenate([lpart[0, rows, :], lpart[1, rows, :]], axis=1)
        lx[x] = lx_send[x]
        for i in range(1, 4):
            send(lx_send.at[wrap(x + i)], lx.at[x], number("LX", i - 1), device(x_=wrap(x + i)))

    def factors_y():
        arrived(rgot, number("RC"))
        for q in range(4):
            lanes = slice(q * RCOLS, (q + 1) * RCOLS)
            ry_send[q] = rpart[:, lanes] + rgot[:, lanes]
        ry[y] = ry_send[y]
        for i in range(1, 4):
            send(ry_send.at[wrap(y + i)], ry.at[y], number("RY", i - 1), device(y_=wrap(y + i)))

    def factors_x():
        for i in range(1, 4):
            arrived(lx.at[wrap(x + 4 - i)], number("LX", i - 1))
        lz[...] = (lx[0] + lx[1]) + (lx[2] + lx[3])
        send(lz, lz_got, number("LZ"), device(zh_=other))

    def factors_z():
        for i in range(1, 4):
            arrived(ry.at[wrap(y + 4 - i)], number("RY", i - 1))
        rz[zl] = (ry[0] + ry[1]) + (ry[2] + ry[3])
        for i in range(1, 4):
            send(rz.at[zl], rz.at[zl], number("RZ", i - 1), device(zl_=wrap(zl + i)))

    def left_share():
        arrived(lz_got, number("LZ"))
        lall[k, x] = lz[...] + lz_got[...]
        for i in range(4):
            for c in range(2):
                if i or c:
                    send(lall.at[k, x], lall.at[k, x], number("LG", 2 * i + c - 1),
                         device(x_=wrap(x + i), k_=k if c == 0 else 1 - k))

    def right_share():
        for i in range(1, 4):
            arrived(rz.at[wrap(zl + 4 - i)], number("RZ", i - 1))
        rall[y] = (rz[0] + rz[1]) + (rz[2] + rz[3])
        for i in range(1, 4):
            send(rall.at[y], rall.at[y], number("RG", i - 1), device(y_=wrap(y + i)))

    def factors_end():
        for i in range(4):
            for c in range(2):
                if i or c:
                    arrived(lall.at[k if c == 0 else 1 - k, wrap(x + 4 - i)], number("LG", 2 * i + c - 1))
        for c in range(2):
            for q in range(4):
                left_out[q * LROWS : (q + 1) * LROWS, c * HALF : (c + 1) * HALF] = lall[c, q]
        for i in range(1, 4):
            arrived(rall.at[wrap(y + 4 - i)], number("RG", i - 1))
        for q in range(4):
            right_out[:, q * RCOLS : (q + 1) * RCOLS] = rall[q]

    zs = (other, zh)

    send_a_x()
    send_g()
    send_sibling()
    merge_own()
    g_from_y(0)
    g_from_z(1)
    g_from_z(3)
    a_forward("AF", "AX", zh, 0)
    a_forward("AF", "AX", zh, 1)
    g_from_z(2)
    send_a_z(0)
    merge_sibling()
    shares(0)
    g_from_y(1)
    g_from_y(3)
    g_from_far(0)
    g_from_y(2)
    g_from_far(1)
    shares(3)
    shares(1)
    g_from_far(3)
    g_from_far(2)
    sent(number("AZ"))
    send_a_z(1)
    a_from_z(0)
    shares(2)
    arrived(a_block(x, zh, 1 - k), number("AS"))
    a_rest(zh, "AX", "AF")
    a_from_z(1)
    pass_on(0, 0)
    pass_on(0, 1)
    a_forward("APF", "AP", other, 0)
    a_forward("APF", "AP", other, 1)
    send_z(0)
    shares_later()
    send_z(1)
    a_rest(other, "AP", "APF")
    factors(0, 2)
    factors_send()
    pass_on(1, 0)
    factors_y()
    pass_on(1, 1)
    factors_x()
    factors_z()

    own_sums(0)
    left_share()
    right_share()
    own_sums(1)
    theirs = pl.multiple_of((1 - k) * TOK, TOK)
    ours = pl.multiple_of(k * TOK, TOK)
    for u in range(2):
        arrived(z_got.at[u], number("Z", u))
        part = slice(u * PIECE, (u + 1) * PIECE)

        def total(first, h):
            sums = p_buf[2, pl.ds(first + u * PIECE, PIECE), :]
            return (sums + z_got[u, pl.ds(pl.multiple_of(h * PIECE, PIECE), PIECE), :].astype(F32)).astype(BF16)

        o_send[part, :] = total(theirs, 1 - k)
        send(o_send.at[part, :], out.at[part, half(k)], number("O", u), sibling)
        o_own[part, :] = total(ours, k)
        pltpu.make_async_copy(o_own.at[part, :], out.at[part, half(k)], local_sem.at[u]).start()
    factors_end()
    for u in range(2):
        part = slice(u * PIECE, (u + 1) * PIECE)
        pltpu.make_async_copy(o_own.at[part, :], out.at[part, half(k)], local_sem.at[u]).wait()
        arrived(out.at[part, half(1 - k)], number("O", u))
    for copy in pending.values():
        copy.wait_send()
    for n in range(8):
        for name in ("S1", "S2"):
            left(s_buf.at[0, pl.ds(0, PIECE), :], number(name, n))


def place(*arrays):
    def move(*refs):
        for src, dst in zip(refs[:3], refs[3:]):
            dst[...] = src[...]

    return pl.pallas_call(
        move,
        out_shape=tuple(jax.ShapeDtypeStruct(v.shape, v.dtype) for v in arrays),
        name="place_results",
    )(*arrays)


def per_device(a, g, w, code, lf, rf):
    anywhere = pl.BlockSpec(memory_space=pl.ANY)
    vmem = pl.BlockSpec(memory_space=pltpu.VMEM)
    out, left, right = pl.pallas_call(
        kernel,
        out_shape=(
            jax.ShapeDtypeStruct((TOK, HID), BF16),
            jax.ShapeDtypeStruct((RANK, HID), F32),
            jax.ShapeDtypeStruct((RANK, COLS), F32),
        ),
        in_specs=[anywhere] * 6,
        out_specs=(anywhere, vmem, vmem),
        scratch_shapes=[
            pltpu.VMEM((TOKENS, HALF), BF16),
            pltpu.VMEM((HALF, TOKENS), BF16),
            pltpu.VMEM((TOKENS, BOTH), BF16),
            pltpu.VMEM((HALF, BOTH), BF16),
            pltpu.VMEM((HALF // 4, BOTH), jnp.int32),
            pltpu.VMEM((RANK, BOTH), BF16),
            pltpu.VMEM((RANK, HALF), BF16),
            pltpu.VMEM((HALF, BOTH), BF16),
            pltpu.VMEM((HALF, BOTH), BF16),
            pltpu.VMEM((4, 4 * TOK, HALF), F32),
            pltpu.VMEM((4, 4 * TOK, HALF), BF16),
            pltpu.VMEM((2, 4 * TOK, HALF), BF16),
            pltpu.VMEM((2, 4 * TOK, HALF), BF16),
            pltpu.VMEM((2, TOK, HALF), BF16),
            pltpu.VMEM((2, TOK, HALF), BF16),
            pltpu.VMEM((TOK, HALF), BF16),
            pltpu.VMEM((TOK, HALF), BF16),
            pltpu.VMEM((2, RANK, HALF // 2), F32),
            pltpu.VMEM((4, LROWS, HALF), F32),
            pltpu.VMEM((4, LROWS, HALF), F32),
            pltpu.VMEM((LROWS, HALF), F32),
            pltpu.VMEM((LROWS, HALF), F32),
            pltpu.VMEM((2, 4, LROWS, HALF), F32),
            pltpu.VMEM((RANK, BOTH), F32),
            pltpu.VMEM((RANK, COLS), F32),
            pltpu.VMEM((4, RANK, RCOLS), F32),
            pltpu.VMEM((4, RANK, RCOLS), F32),
            pltpu.VMEM((4, RANK, RCOLS), F32),
            pltpu.VMEM((4, RANK, RCOLS), F32),
            pltpu.SemaphoreType.DMA((COPIES,)),
            pltpu.SemaphoreType.DMA((COPIES,)),
            pltpu.SemaphoreType.DMA((6,)),
        ],
        compiler_params=pltpu.CompilerParams(
            collective_id=0, has_side_effects=True, vmem_limit_bytes=58 << 20
        ),
        cost_estimate=pl.CostEstimate(flops=7_600_000_000, bytes_accessed=5_000_000, transcendentals=0),
        name="down_projection_backward",
    )(a, g, w, code, lf.T, rf)
    out, left, right = place(out, left, right)
    return out, left.T, right


def solution(mesh):
    in_specs = (
        P("col", "row"),
        P("row", "col"),
        P("row", "col"),
        P("row", "col"),
        P("row", None),
        P(None, "col"),
    )
    out_specs = (P("col", "row"), P("row", None), P(None, "col"))
    return jax.shard_map(
        per_device, mesh=mesh, in_specs=in_specs, out_specs=out_specs, check_vma=False
    )
```

```python
import functools

import jax
import jax.numpy as jnp
from jax import lax
from jax.experimental import pallas as pl
from jax.experimental.pallas import tpu as pltpu
from jax.sharding import PartitionSpec as P

MESH = pl.DeviceIdType.MESH
BF16, F32 = jnp.bfloat16, jnp.float32
TOKENS, RANK = 2048, 16
TOK, HID, COLS = 128, 1792, 512
HALF, BOTH = HID // 2, 2 * COLS
NT = (((1,), (1,)), ((), ()))
TN = (((0,), (0,)), ((), ()))
HT = 128
PIECE = TOK // 2
LROWS, RCOLS = RANK // 4, COLS // 4
WIDE = ((0, 256), (256, 256), (512, 256), (768, 128))

NUMBERS = {}


def numbered(name, count):
    NUMBERS[name] = sum(c for _, c in NUMBERS.values()), count


for _name, _count in (
    ("AX", 4), ("AZ", 2), ("AS", 1), ("AF", 2), ("AP", 4), ("APF", 2),
    ("GZ", 3), ("GY", 8), ("GF", 4), ("GS", 16),
    ("W", 1), ("C", 1), ("R", 1),
    ("S1", 8), ("S2", 8), ("S3", 8), ("Z", 2), ("O", 2),
    ("LX", 3), ("LZ", 1), ("LG", 7), ("RC", 1), ("RY", 3), ("RZ", 3), ("RG", 3),
):
    numbered(_name, _count)
COPIES = sum(c for _, c in NUMBERS.values())


def number(name, index=0):
    return NUMBERS[name][0] + index


def merge_tiles(slot, w_buf, c_buf, r_buf, l_buf, mask_buf, m_buf):
    cols = pl.ds(slot * COLS, COLS)
    groups = HT // 4
    row = lax.broadcasted_iota(jnp.int32, (HT, HT), 0)
    lane = lax.broadcasted_iota(jnp.int32, (HT, HT), 1)
    hit = (row % 4 == lane // groups) & (row // 4 == lane % groups)
    spread = jnp.where(hit, 1.0, 0.0).astype(BF16)
    right = r_buf[:, cols]

    def tile(i, _):
        code = c_buf[pl.ds(pl.multiple_of(i * groups, groups), groups), cols]
        is0, is1, is2 = code == 0, code == 1, code == 2
        is3, is4, is5 = code == 3, code == 4, code == 5
        kept = (is0 | is1 | is2, is0 | is3 | is4, is1 | is3 | is5, is2 | is4 | is5)
        kept = jnp.concatenate([jnp.where(b, 1.0, 0.0) for b in kept], axis=0).astype(BF16)
        mask = jnp.dot(spread, kept, preferred_element_type=F32)
        rows = pl.ds(pl.multiple_of(i * HT, HT), HT)
        low = lax.dot_general(l_buf[:, rows], right, TN, preferred_element_type=F32)
        merged = mask * (w_buf[rows, cols].astype(F32) + 2.0 * low)
        mask_buf[rows, cols] = mask.astype(BF16)
        m_buf[rows, cols] = merged.astype(BF16)
        return 0

    lax.fori_loop(0, HALF // HT, tile, 0)


def product(i, x_dest, g_buf, m_buf, p_buf):
    first = pl.multiple_of(x_dest * 4 * TOK, 4 * TOK)
    for at, size in WIDE:
        p_buf[i, :, at : at + size] = lax.dot_general(
            g_buf[pl.ds(first, 4 * TOK), :], m_buf[at : at + size, :], NT, preferred_element_type=F32
        )


def turn(a_buf, at_buf, zh):
    def block(i, _):
        toks = pl.ds(pl.multiple_of(((i // 2) * 4 + zh * 2 + i % 2) * TOK, TOK), TOK)
        at_buf[:, toks] = a_buf[toks, :].T
        return 0

    lax.fori_loop(0, TOKENS // TOK // 2, block, 0)


def factor_grads(first, last, at_buf, g_buf, mask_buf, r_buf, l_buf, left, right):
    if first == 0:
        left[...] = jnp.zeros_like(left)
    step = 512

    def tile(n, _):
        cols = pl.ds(pl.multiple_of(n * step, step), step)
        total = jnp.zeros((RANK, step), F32)
        for half in range(2):
            rows = pl.ds(half * (HALF // 2), HALF // 2)
            grad = jnp.dot(at_buf[rows, :], g_buf[:, cols], preferred_element_type=F32)
            pruned = (mask_buf[rows, cols].astype(F32) * grad * (1.0 / TOKENS)).astype(BF16)
            total += jnp.dot(l_buf[:, rows], pruned, preferred_element_type=F32)
            left[half] += 2.0 * lax.dot_general(
                r_buf[:, cols], pruned, NT, preferred_element_type=F32
            )
        right[:, cols] = 2.0 * total
        return 0

    lax.fori_loop(first, last, tile, 0)


def kernel(
    a, g, w, code, lf, rf, out, left_out, right_out,
    a_buf, at_buf, g_buf, w_buf, c_buf, r_buf, l_buf, mask_buf, m_buf,
    p_buf, s_buf, got1, got2, z_send, z_got, o_send, o_own,
    lpart, lx_send, lx, lz, lz_got, lall, rpart, rgot, ry_send, ry, rz, rall,
    send_sem, recv_sem, local_sem,
):
    row, col = lax.axis_index("row"), lax.axis_index("col")
    y, zl = row // 4, row % 4
    x, zh, k = col // 4, (col // 2) % 2, col % 2
    other = 1 - zh

    def device(y_=y, zl_=zl, x_=x, zh_=zh, k_=k):
        return (y_ * 4 + zl_, x_ * 4 + zh_ * 2 + k_)

    def wrap(v):
        return v % 4

    x_at = (wrap(x + 1), wrap(x + 3))
    y_at = (wrap(y + 1), wrap(y + 3))
    sibling = device(k_=1 - k)
    peers = [sibling]
    peers += [device(x_=x_at[d], k_=j) for d in range(2) for j in range(2)]
    peers += [device(x_=wrap(x + 2), k_=j) for j in range(2)]
    peers += [device(zh_=other, k_=j) for j in range(2)]
    peers += [device(y_=wrap(y + i)) for i in range(1, 4)]
    peers += [device(zl_=wrap(zl + i)) for i in range(1, 4)]

    pending = {}

    def send(src, dst, n, to, recv_n=None, keep=True):
        copy = pltpu.make_async_remote_copy(
            src_ref=src, dst_ref=dst, send_sem=send_sem.at[n],
            recv_sem=recv_sem.at[n if recv_n is None else recv_n],
            device_id=to, device_id_type=MESH,
        )
        copy.start()
        if keep:
            pending[n] = copy

    def arrived(dst, n):
        pltpu.make_async_remote_copy(
            src_ref=dst, dst_ref=dst, send_sem=send_sem.at[n], recv_sem=recv_sem.at[n],
            device_id=sibling, device_id_type=MESH,
        ).wait_recv()

    def left(src, n):
        pltpu.make_async_remote_copy(
            src_ref=src, dst_ref=src, send_sem=send_sem.at[n], recv_sem=recv_sem.at[n],
            device_id=sibling, device_id_type=MESH,
        ).wait_send()

    def sent(n):
        pending.pop(n).wait_send()

    def tokens_of(x_, zh_, k_):
        return pl.ds(pl.multiple_of((x_ * 4 + zh_ * 2 + k_) * TOK, TOK), TOK)

    def a_block(x_, zh_, k_):
        return a_buf.at[tokens_of(x_, zh_, k_), :]

    def g_block(y_, zl_, slot=0):
        return g_buf.at[pl.ds(pl.multiple_of((y_ * 4 + zl_) * TOK, TOK), TOK), pl.ds(slot * COLS, COLS)]

    def half(j):
        return pl.ds(pl.multiple_of(j * HALF, HALF), HALF)

    def quarter(j):
        return pl.ds(pl.multiple_of(j * (HALF // 4), HALF // 4), HALF // 4)

    own_cols, sib_cols = pl.ds(0, COLS), pl.ds(COLS, COLS)

    locals_ = [
        pltpu.make_async_copy(src, dst, local_sem.at[n])
        for n, (src, dst) in enumerate((
            (w.at[half(k), :], w_buf.at[:, own_cols]),
            (code.at[quarter(k), :], c_buf.at[:, own_cols]),
            (lf.at[:, half(k)], l_buf),
            (rf, r_buf.at[:, own_cols]),
            (a.at[:, half(k)], a_block(x, zh, k)),
            (g, g_block(y, zl)),
        ))
    ]
    for copy in locals_:
        copy.start()

    barrier = pltpu.get_barrier_semaphore()
    for peer in peers:
        pl.semaphore_signal(barrier, inc=1, device_id=peer, device_id_type=MESH)
    pl.semaphore_wait(barrier, len(peers))

    def send_a_x():
        for j in range(2):
            for d in range(2):
                send(a.at[:, half(j)], a_block(x, zh, k), number("AX", 2 * d + j), device(x_=x_at[d], k_=j),
                     number("AX", 2 * d) + k)

    def send_g():
        for d in range(2):
            send(g, g_block(y, zl), number("GY", 4 * d), device(y_=y_at[d]))
        for i in (1, 3, 2):
            send(g, g_block(y, zl), number("GZ", i - 1), device(zl_=wrap(zl + i)))

    def send_a_z(i):
        j = k if i == 0 else 1 - k
        send(a.at[:, half(j)], a_block(x, zh, k), number("AZ", i), device(zh_=other, k_=j), number("AZ") + k)

    def send_sibling():
        send(g, g_block(y, zl, 1), number("GS"), sibling)
        send(rf, r_buf.at[:, sib_cols], number("R"), sibling)
        send(code.at[quarter(1 - k), :], c_buf.at[:, sib_cols], number("C"), sibling)
        send(w.at[half(1 - k), :], w_buf.at[:, sib_cols], number("W"), sibling)
        send(a.at[:, half(1 - k)], a_block(x, zh, k), number("AS"), sibling)

    def merge_own():
        for copy in locals_:
            copy.wait()
        merge_tiles(0, w_buf, c_buf, r_buf, l_buf, mask_buf, m_buf)

    def merge_sibling():
        for name, ref in (("R", r_buf), ("C", c_buf), ("W", w_buf)):
            arrived(ref.at[:, sib_cols], number(name))
        merge_tiles(1, w_buf, c_buf, r_buf, l_buf, mask_buf, m_buf)

    def g_to_sibling(n, y_, zl_):
        send(g_block(y_, zl_), g_block(y_, zl_, 1), number("GS", n), sibling)

    def a_forward(name, base, zh_, d):
        block = a_block(x_at[1 - d], zh_, d)
        arrived(block, number(base, 2 * d + d))
        send(block, block, number(name, d), device(x_=x_at[d]))

    def a_from_z(i):
        o = k if i == 0 else 1 - k
        block = a_block(x, other, o)
        arrived(block, number("AZ") + o)
        for d in range(2):
            send(block, block, number("AP", 2 * d + i), device(x_=x_at[d]), number("AP", 2 * d) + o)

    def g_from_z(i):
        block = g_block(y, wrap(zl + 4 - i))
        arrived(block, number("GZ", i - 1))
        for d in range(2):
            send(block, block, number("GY", 4 * d + i), device(y_=y_at[d]))
        g_to_sibling(i, y, wrap(zl + 4 - i))

    def g_from_y(i):
        for d in (i % 2, 1 - i % 2):
            from_y, from_zl = y_at[1 - d], wrap(zl + 4 - i)
            block = g_block(from_y, from_zl)
            arrived(block, number("GY", 4 * d + i))
            if i % 2 == d:
                send(block, block, number("GF", i), device(y_=y_at[d]))
            g_to_sibling(4 + 4 * d + i, from_y, from_zl)

    def g_from_far(i):
        block = g_block(wrap(y + 2), wrap(zl + 4 - i))
        arrived(block, number("GF", i))
        g_to_sibling(12 + i, wrap(y + 2), wrap(zl + 4 - i))

    def g_row(e):
        first = {0: 0, 3: 4, 1: 8, 2: 12}[e]
        for i in range(4):
            arrived(g_block(wrap(y + e), wrap(zl + 4 - i), 1), number("GS", first + i))

    def piece(zh_, h, u):
        return pl.ds(pl.multiple_of(zh_ * 2 * TOK + h * TOK + u * PIECE, PIECE), PIECE)

    def share_number(name, zh_, u, d):
        return number(name) + (zh_ * 4 + u * 2 + d)

    def send_far(q, u):
        zh_ = zs[q]
        for d in range(2):
            rows = piece(zh_, d, u)
            s_buf[2, rows, :] = p_buf[2, rows, :].astype(BF16)
            send(s_buf.at[2, rows, :], got1.at[d, rows, :], number("S1", 4 * q + 2 * u + d),
                 device(x_=x_at[d]), share_number("S1", zh_, u, d), keep=False)

    def send_near(q, u, d):
        zh_ = zs[q]
        rows = piece(zh_, 1 - d, u)
        to = 1 + 2 * d
        s_buf[to, rows, :] = p_buf[to, rows, :].astype(BF16)
        send(s_buf.at[to, rows, :], got2.at[d, rows, :], number("S2", 4 * q + 2 * u + d),
             device(x_=x_at[d]), share_number("S2", zh_, u, d), keep=False)

    def shares(e):
        g_row(e)
        place_ = wrap(y + e + 4 - x)
        product(place_, wrap(y + e), g_buf, m_buf, p_buf)
        early = (0, 1) if e == 0 else (0,)

        @pl.when(place_ == 2)
        def _():
            for q in early:
                for u in range(2):
                    send_far(q, u)

        for d in range(2):

            @pl.when(place_ == 1 + 2 * d)
            def _():
                for q in early:
                    for u in range(2):
                        send_near(q, u, d)

    def shares_later():
        place_ = wrap(y + 4 - x)

        @pl.when(place_ != 2)
        def _():
            for u in range(2):
                send_far(1, u)

        for d in range(2):

            @pl.when(place_ != 1 + 2 * d)
            def _():
                for u in range(2):
                    send_near(1, u, d)

    def pass_on(q, u):
        zh_ = zs[q]
        for d in range(2):
            rows = piece(zh_, d, u)
            arrived(got1.at[d, rows, :], share_number("S1", zh_, u, d))
            to = 1 + 2 * d
            s_buf[to, rows, :] = (p_buf[to, rows, :] + got1[d, rows, :].astype(F32)).astype(BF16)
            send(s_buf.at[to, rows, :], got2.at[d, rows, :], number("S3", 4 * q + 2 * u + d),
                 device(x_=x_at[d]), share_number("S3", zh_, u, d))

    def summed(q, u, h):
        zh_ = zs[q]
        rows = piece(zh_, h, u)
        for d in range(2):
            arrived(got2.at[d, rows, :], share_number("S3" if h == d else "S2", zh_, u, d))
        return p_buf[0, rows, :] + got2[0, rows, :].astype(F32) + got2[1, rows, :].astype(F32)

    def send_z(u):
        for h in range(2):
            z_send[u, h * PIECE : (h + 1) * PIECE, :] = summed(0, u, h).astype(BF16)
        send(z_send.at[u], z_got.at[u], number("Z", u), device(zh_=other))

    def own_sums(u):
        for h in range(2):
            p_buf[2, h * TOK + u * PIECE : h * TOK + (u + 1) * PIECE, :] = summed(1, u, h)

    def a_rest(zh_, near, far):
        for d in range(2):
            arrived(a_block(x_at[1 - d], zh_, 1 - d), number(near, 2 * d + 1 - d))
            arrived(a_block(wrap(x + 2), zh_, d), number(far, d))
        turn(a_buf, at_buf, zh_)

    def factors(first, last):
        factor_grads(first, last, at_buf, g_buf, mask_buf, r_buf, l_buf, lpart, rpart)

    def factors_send():
        send(rpart.at[:, sib_cols], rgot, number("RC"), sibling)
        for q in range(4):
            rows = slice(q * LROWS, (q + 1) * LROWS)
            lx_send[q] = jnp.concatenate([lpart[0, rows, :], lpart[1, rows, :]], axis=1)
        lx[x] = lx_send[x]
        for i in range(1, 4):
            send(lx_send.at[wrap(x + i)], lx.at[x], number("LX", i - 1), device(x_=wrap(x + i)))

    def factors_y():
        arrived(rgot, number("RC"))
        for q in range(4):
            lanes = slice(q * RCOLS, (q + 1) * RCOLS)
            ry_send[q] = rpart[:, lanes] + rgot[:, lanes]
        ry[y] = ry_send[y]
        for i in range(1, 4):
            send(ry_send.at[wrap(y + i)], ry.at[y], number("RY", i - 1), device(y_=wrap(y + i)))

    def factors_x():
        for i in range(1, 4):
            arrived(lx.at[wrap(x + 4 - i)], number("LX", i - 1))
        lz[...] = (lx[0] + lx[1]) + (lx[2] + lx[3])
        send(lz, lz_got, number("LZ"), device(zh_=other))

    def factors_z():
        for i in range(1, 4):
            arrived(ry.at[wrap(y + 4 - i)], number("RY", i - 1))
        rz[zl] = (ry[0] + ry[1]) + (ry[2] + ry[3])
        for i in range(1, 4):
            send(rz.at[zl], rz.at[zl], number("RZ", i - 1), device(zl_=wrap(zl + i)))

    def left_share():
        arrived(lz_got, number("LZ"))
        lall[k, x] = lz[...] + lz_got[...]
        for i in range(4):
            for c in range(2):
                if i or c:
                    send(lall.at[k, x], lall.at[k, x], number("LG", 2 * i + c - 1),
                         device(x_=wrap(x + i), k_=k if c == 0 else 1 - k))

    def right_share():
        for i in range(1, 4):
            arrived(rz.at[wrap(zl + 4 - i)], number("RZ", i - 1))
        rall[y] = (rz[0] + rz[1]) + (rz[2] + rz[3])
        for i in range(1, 4):
            send(rall.at[y], rall.at[y], number("RG", i - 1), device(y_=wrap(y + i)))

    def factors_end():
        for i in range(4):
            for c in range(2):
                if i or c:
                    arrived(lall.at[k if c == 0 else 1 - k, wrap(x + 4 - i)], number("LG", 2 * i + c - 1))
        for c in range(2):
            for q in range(4):
                left_out[q * LROWS : (q + 1) * LROWS, c * HALF : (c + 1) * HALF] = lall[c, q]
        for i in range(1, 4):
            arrived(rall.at[wrap(y + 4 - i)], number("RG", i - 1))
        for q in range(4):
            right_out[:, q * RCOLS : (q + 1) * RCOLS] = rall[q]

    zs = (other, zh)

    send_a_x()
    send_g()
    send_sibling()
    merge_own()
    g_from_y(0)
    g_from_z(1)
    g_from_z(3)
    a_forward("AF", "AX", zh, 0)
    a_forward("AF", "AX", zh, 1)
    g_from_z(2)
    send_a_z(0)
    merge_sibling()
    shares(0)
    g_from_y(1)
    g_from_y(3)
    g_from_far(0)
    g_from_y(2)
    g_from_far(1)
    shares(3)
    shares(1)
    g_from_far(3)
    g_from_far(2)
    sent(number("AZ"))
    send_a_z(1)
    a_from_z(0)
    shares(2)
    arrived(a_block(x, zh, 1 - k), number("AS"))
    a_rest(zh, "AX", "AF")
    a_from_z(1)
    pass_on(0, 0)
    pass_on(0, 1)
    a_forward("APF", "AP", other, 0)
    a_forward("APF", "AP", other, 1)
    send_z(0)
    shares_later()
    send_z(1)
    a_rest(other, "AP", "APF")
    factors(0, 2)
    factors_send()
    pass_on(1, 0)
    factors_y()
    pass_on(1, 1)
    factors_x()
    factors_z()

    left_share()
    own_sums(0)
    right_share()
    own_sums(1)
    theirs = pl.multiple_of((1 - k) * TOK, TOK)
    ours = pl.multiple_of(k * TOK, TOK)
    for u in range(2):
        arrived(z_got.at[u], number("Z", u))
        part = slice(u * PIECE, (u + 1) * PIECE)

        def total(first, h):
            sums = p_buf[2, pl.ds(first + u * PIECE, PIECE), :]
            return (sums + z_got[u, pl.ds(pl.multiple_of(h * PIECE, PIECE), PIECE), :].astype(F32)).astype(BF16)

        o_send[part, :] = total(theirs, 1 - k)
        send(o_send.at[part, :], out.at[part, half(k)], number("O", u), sibling)
        o_own[part, :] = total(ours, k)
        pltpu.make_async_copy(o_own.at[part, :], out.at[part, half(k)], local_sem.at[u]).start()
    factors_end()
    for u in range(2):
        part = slice(u * PIECE, (u + 1) * PIECE)
        pltpu.make_async_copy(o_own.at[part, :], out.at[part, half(k)], local_sem.at[u]).wait()
        arrived(out.at[part, half(1 - k)], number("O", u))
    for copy in pending.values():
        copy.wait_send()
    for n in range(8):
        for name in ("S1", "S2"):
            left(s_buf.at[0, pl.ds(0, PIECE), :], number(name, n))


def place(*arrays):
    def move(*refs):
        for src, dst in zip(refs[:3], refs[3:]):
            dst[...] = src[...]

    return pl.pallas_call(
        move,
        out_shape=tuple(jax.ShapeDtypeStruct(v.shape, v.dtype) for v in arrays),
        name="place_results",
    )(*arrays)


def per_device(a, g, w, code, lf, rf):
    anywhere = pl.BlockSpec(memory_space=pl.ANY)
    vmem = pl.BlockSpec(memory_space=pltpu.VMEM)
    out, left, right = pl.pallas_call(
        kernel,
        out_shape=(
            jax.ShapeDtypeStruct((TOK, HID), BF16),
            jax.ShapeDtypeStruct((RANK, HID), F32),
            jax.ShapeDtypeStruct((RANK, COLS), F32),
        ),
        in_specs=[anywhere] * 6,
        out_specs=(anywhere, vmem, vmem),
        scratch_shapes=[
            pltpu.VMEM((TOKENS, HALF), BF16),
            pltpu.VMEM((HALF, TOKENS), BF16),
            pltpu.VMEM((TOKENS, BOTH), BF16),
            pltpu.VMEM((HALF, BOTH), BF16),
            pltpu.VMEM((HALF // 4, BOTH), jnp.int32),
            pltpu.VMEM((RANK, BOTH), BF16),
            pltpu.VMEM((RANK, HALF), BF16),
            pltpu.VMEM((HALF, BOTH), BF16),
            pltpu.VMEM((HALF, BOTH), BF16),
            pltpu.VMEM((4, 4 * TOK, HALF), F32),
            pltpu.VMEM((4, 4 * TOK, HALF), BF16),
            pltpu.VMEM((2, 4 * TOK, HALF), BF16),
            pltpu.VMEM((2, 4 * TOK, HALF), BF16),
            pltpu.VMEM((2, TOK, HALF), BF16),
            pltpu.VMEM((2, TOK, HALF), BF16),
            pltpu.VMEM((TOK, HALF), BF16),
            pltpu.VMEM((TOK, HALF), BF16),
            pltpu.VMEM((2, RANK, HALF // 2), F32),
            pltpu.VMEM((4, LROWS, HALF), F32),
            pltpu.VMEM((4, LROWS, HALF), F32),
            pltpu.VMEM((LROWS, HALF), F32),
            pltpu.VMEM((LROWS, HALF), F32),
            pltpu.VMEM((2, 4, LROWS, HALF), F32),
            pltpu.VMEM((RANK, BOTH), F32),
            pltpu.VMEM((RANK, COLS), F32),
            pltpu.VMEM((4, RANK, RCOLS), F32),
            pltpu.VMEM((4, RANK, RCOLS), F32),
            pltpu.VMEM((4, RANK, RCOLS), F32),
            pltpu.VMEM((4, RANK, RCOLS), F32),
            pltpu.SemaphoreType.DMA((COPIES,)),
            pltpu.SemaphoreType.DMA((COPIES,)),
            pltpu.SemaphoreType.DMA((6,)),
        ],
        compiler_params=pltpu.CompilerParams(
            collective_id=0, has_side_effects=True, vmem_limit_bytes=58 << 20
        ),
        cost_estimate=pl.CostEstimate(flops=7_600_000_000, bytes_accessed=5_000_000, transcendentals=0),
        name="down_projection_backward",
    )(a, g, w, code, lf.T, rf)
    out, left, right = place(out, left, right)
    return out, left.T, right


def solution(mesh):
    in_specs = (
        P("col", "row"),
        P("row", "col"),
        P("row", "col"),
        P("row", "col"),
        P("row", None),
        P(None, "col"),
    )
    out_specs = (P("col", "row"), P("row", None), P(None, "col"))
    return jax.shard_map(
        per_device, mesh=mesh, in_specs=in_specs, out_specs=out_specs, check_vma=False
    )
```
